128 devices in a mesh: tm: 8 (over z, core), rows: 16 (over y, x).
Axes of the slice: x: 4, y: 4, z: 4, core: 2. Of those that a mesh axis runs over, the one named last changes fastest.
Arguments:
- latent: bfloat16 [16, 32, 48, 512], P('tm', 'rows'), may hold values from -24 to 24, as said below
- gain_first: float32 [512], replicated, may hold values from 0.1 to 1.9
- shift_first: float32 [512], replicated, may hold values from -0.5 to 0.5
- kernel_first: bfloat16 [3, 3, 3, 512, 256], replicated, may hold values from -0.0546875 to 0.0546875
- gain_second: float32 [256], replicated, may hold values from 0.1 to 1.9
- shift_second: float32 [256], replicated, may hold values from -0.5 to 0.5
- kernel_second: bfloat16 [3, 3, 3, 256, 256], replicated, may hold values from -0.078125 to 0.078125
Outputs:
- decoded: bfloat16 [32, 64, 96, 256], P('tm', 'rows')
The draws below stay inside these ranges and needn't reach their ends.
Inputs may be any that keep to these rules, and one draw needn't show every extreme that they name: `latent`: real-valued features.
All inputs are finite; a program needn't handle non-finite values.
Results may differ from the reference program's by a relative error of at most 0.015.
Values may be sent and summed in bfloat16 or wider, within the bound.
A program may use at most 64 MiB of HBM per device.

```python
import jax
import jax.numpy as jnp
from jax import lax

CIN = 512
COUT = 256
GROUPS = 32
WIDTH = 48
FRAMES = 16
ROWS = 32


def draw_latent(key, part):
    key = jax.random.fold_in(key, 11)
    keys = jax.random.split(key, 7)
    shape = (FRAMES, ROWS, WIDTH, CIN)
    frame_pos = jnp.arange(FRAMES, dtype=jnp.float32)[:, None, None, None]
    row_pos = jnp.arange(ROWS, dtype=jnp.float32)[None, :, None, None]
    frame_factor = jax.random.uniform(keys[3], (FRAMES, 1, 1, 1), jnp.float32, 0.6, 1.4)
    row_factor = jax.random.uniform(keys[4], (1, ROWS, 1, 1), jnp.float32, 0.6, 1.4)
    ramp = jnp.power(3.0, frame_pos / max(FRAMES - 1, 1)) * jnp.power(3.0, row_pos / max(ROWS - 1, 1))
    ramp = ramp * frame_factor * row_factor
    base = jax.random.normal(keys[0], shape, jnp.float32)
    base = jnp.clip(base, -4.0, 4.0)
    offset = jax.random.uniform(keys[1], (CIN,), jnp.float32, -0.5, 0.5)
    drift_frame = jax.random.uniform(keys[5], (FRAMES, 1, 1, 1), jnp.float32, -1.5, 1.5)
    drift_group = jnp.repeat(jax.random.uniform(keys[6], (GROUPS,), jnp.float32, -1.0, 1.0), CIN // GROUPS)
    rough = jax.random.uniform(keys[2], (1, ROWS, WIDTH, 1), jnp.float32, 0.5, 1.0)
    return ((base + offset + drift_frame * drift_group) * ramp * rough / 5.0).astype(jnp.bfloat16)


def bell_draw(key, dims, scale, bound, kind=jnp.bfloat16):
    array = scale * jax.random.normal(key, dims, jnp.float32)
    return jnp.clip(array, min=-bound, max=bound).astype(kind)


def setup_inputs(seed: int = 0) -> dict:
    key_list = jax.random.split(jax.random.key(seed), 8)
    latent = draw_latent(jax.random.fold_in(key_list[7], 71), 0)
    gain_first = jnp.clip(1.0 + 0.18 * jax.random.normal(key_list[1], (CIN,), jnp.float32), 0.1, 1.9)
    shift_first = jnp.clip(jax.random.uniform(key_list[2], (CIN,), jnp.float32, -0.5, 0.5), -0.5, 0.5)
    kernel_first = bell_draw(key_list[3], (3, 3, 3, CIN, COUT), (27 * CIN) ** -0.5, 0.0546875)
    gain_second = jnp.clip(1.0 + 0.18 * jax.random.normal(key_list[4], (COUT,), jnp.float32), 0.1, 1.9)
    shift_second = jnp.clip(jax.random.uniform(key_list[5], (COUT,), jnp.float32, -0.5, 0.5), -0.5, 0.5)
    kernel_second = bell_draw(key_list[6], (3, 3, 3, COUT, COUT), (27 * COUT) ** -0.5, 0.078125)
    return {"latent": latent, "gain_first": gain_first, "shift_first": shift_first, "kernel_first": kernel_first, "gain_second": gain_second, "shift_second": shift_second, "kernel_second": kernel_second}


EPS = 1e-06

def channel_stats(values, groups):
    chans = values.shape[-1]
    flat = values.reshape(-1, chans)
    total = lax.optimization_barrier(jnp.sum(flat, axis=0)).reshape(groups, -1).sum(axis=1)
    square = lax.optimization_barrier(jnp.sum(flat * flat, axis=0)).reshape(groups, -1).sum(axis=1)
    return (total, square)

def normalize(values, total, square, count, gain, shift, groups):
    chans = values.shape[-1]
    mean = total / count
    spread = square / count - mean * mean
    scale = lax.rsqrt(spread + EPS)
    mean_c = jnp.repeat(mean, chans // groups)
    scale_c = jnp.repeat(scale, chans // groups)
    inner = (values.astype(jnp.float32) - mean_c) * scale_c * gain + shift
    return jax.nn.silu(inner).astype(jnp.bfloat16)

def convolve(padded, kernel, frames, height, width):
    cin = padded.shape[-1]
    cout = kernel.shape[-1]
    total = jnp.zeros((frames * height * width, cout), jnp.float32)
    for ta in range(3):
        for hb in range(3):
            for wc in range(3):
                piece = padded[ta:ta + frames, hb:hb + height, wc:wc + width].reshape(-1, cin)
                total = total + jnp.dot(piece, kernel[ta, hb, wc], preferred_element_type=jnp.float32)
    return total.reshape(frames, height, width, cout)

def upsample(values):
    values = jnp.repeat(values, 2, axis=0)
    values = jnp.repeat(values, 2, axis=1)
    return jnp.repeat(values, 2, axis=2)

def reference(latent, gain_first, shift_first, kernel_first, gain_second, shift_second, kernel_second):
    total, square = channel_stats(latent.astype(jnp.float32), GROUPS)
    count = FRAMES * ROWS * WIDTH * (CIN // GROUPS)
    first = normalize(latent, total, square, count, gain_first, shift_first, GROUPS)
    padded = jnp.pad(first, ((2, 0), (1, 1), (1, 1), (0, 0)))
    middle = convolve(padded, kernel_first, FRAMES, ROWS, WIDTH).astype(jnp.bfloat16)
    total, square = channel_stats(middle.astype(jnp.float32), GROUPS)
    count = FRAMES * ROWS * WIDTH * (COUT // GROUPS)
    second = normalize(middle, total, square, count, gain_second, shift_second, GROUPS)
    upsampled = upsample(second)
    padded = jnp.pad(upsampled, ((2, 0), (1, 1), (1, 1), (0, 0)))
    return convolve(padded, kernel_second, 2 * FRAMES, 2 * ROWS, 2 * WIDTH).astype(jnp.bfloat16)
```

```python
import functools

import jax
import jax.numpy as jnp
from jax import lax
from jax.experimental import pallas as pl
from jax.experimental.pallas import tpu as pltpu
from jax.sharding import PartitionSpec as P

GROUPS = 32
EPS = 1e-06
MESH = pl.DeviceIdType.MESH
LANES = 128
TAPS = 3
CORES = 2
SIDE = 4


def chip_partners(tm, row, tm_n, rows_n):
    at_z = [lax.rem(tm + CORES * d, tm_n) for d in range(tm_n // CORES)]
    at_y = [lax.rem(row - lax.rem(row, SIDE) + SIDE * d, rows_n) for d in range(rows_n // SIDE)]
    at_x = [lax.rem(row + d, SIDE) for d in range(SIDE)]
    hops = lambda d, n: min(d, n - d)
    steps = [
        (-hops(dz, len(at_z)) - hops(dy, len(at_y)) - hops(dx, SIDE), dz, dy, dx)
        for dz in range(len(at_z))
        for dy in range(len(at_y))
        for dx in range(SIDE)
        if dz or dy or dx
    ]
    return [(at_z[dz], at_y[dy] + at_x[dx]) for _, dz, dy, dx in sorted(steps)]


def lane_sums(x, size):
    lane = lax.broadcasted_iota(jnp.int32, x.shape, 1)
    d = 1
    while d < size:
        other = jnp.where((lane & d) == 0, pltpu.roll(x, LANES - d, 1), pltpu.roll(x, d, 1))
        x = x + other
        d *= 2
    return x


def diagonal(size):
    lane = lax.broadcasted_iota(jnp.int32, (8, LANES), 1)
    sub = lax.broadcasted_iota(jnp.int32, (8, LANES), 0)
    return (lane & (size - 1)) == sub


def pack_stats(total, square):
    blocks = total.shape[1] // LANES
    size = total.shape[1] // GROUPS
    sub = lax.broadcasted_iota(jnp.int32, (8, LANES), 0)
    rows = jnp.zeros((8, LANES), jnp.float32)
    for v in range(blocks):
        part = slice(v * LANES, (v + 1) * LANES)
        rows = jnp.where(sub == v, total[:, part], rows)
        rows = jnp.where(sub == blocks + v, square[:, part], rows)
    rows = lane_sums(rows, size)
    return jnp.sum(jnp.where(diagonal(size), rows, 0.0), axis=0, keepdims=True)


def affine(packed, count, gain, shift):
    chans = gain.shape[1]
    blocks, size = chans // LANES, chans // GROUPS
    rows = jnp.where(diagonal(size), jnp.broadcast_to(packed, (8, LANES)), 0.0)
    rows = lane_sums(rows, size) * (1.0 / count)
    mean = rows
    spread = pltpu.roll(rows, 8 - blocks, 0) - mean * mean
    scale = lax.rsqrt(spread + EPS) * 0.5
    a = jnp.concatenate([scale[v : v + 1] for v in range(blocks)], axis=1) * gain
    m = jnp.concatenate([mean[v : v + 1] for v in range(blocks)], axis=1)
    return a, shift * 0.5 - m * a


def activate(x, a, b):
    half = x.astype(jnp.float32) * a + b
    return (half + half * jnp.tanh(half)).astype(jnp.bfloat16)


def kernel(
    tm_n, rows_n,
    latent, gain1, shift1, kernel1, gain2, shift2, kernel2, out,
    lx, xn, w1, w2, w2m, mx, sn, stage, ob, g1, s1, g2, s2, red_core, red_chip,
    load_sem, w1_sem, w2_sem, out_sem, hs_sem, hr_sem, rs_sem, rr_sem,
):
    tm, row = lax.axis_index("tm"), lax.axis_index("rows")
    frames, height, width, cin = latent.shape
    cout = kernel1.shape[-1]
    up_ok, down_ok = row > 0, row < rows_n - 1
    prev_ok, next_ok = tm > 0, tm < tm_n - 1
    tm_at = lambda d: lax.rem(tm + d + tm_n, tm_n)
    row_at = lambda d: lax.rem(row + d + rows_n, rows_n)

    own = lx.at[2:4, 1:3]
    load = pltpu.make_async_copy(latent, own, load_sem.at[0])
    load.start()
    small = [
        pltpu.make_async_copy(src, dst, load_sem.at[1 + n])
        for n, (src, dst) in enumerate(((gain1, g1), (shift1, s1), (gain2, g2), (shift2, s2)))
    ]
    for c in small:
        c.start()
    slot = (0, 4, 2)
    w2_loads, w1_loads = [], []
    for i in range(TAPS):
        w2_loads.append(pltpu.make_async_copy(kernel2.at[i, 0], w2.at[0, :, slot[i]], w2_sem.at[3 * i]))
        w2_loads.append(pltpu.make_async_copy(kernel2.at[i, 1], w2m.at[i], w2_sem.at[3 * i + 1]))
        w2_loads.append(pltpu.make_async_copy(kernel2.at[i, 2], w2.at[1, :, slot[i] + 1], w2_sem.at[3 * i + 2]))
    for i in range(TAPS):
        for k in range(TAPS):
            w1_loads.append(pltpu.make_async_copy(kernel1.at[i, :, k], w1.at[k, i], w1_sem.at[TAPS * i + k]))
    for c in w2_loads + w1_loads:
        c.start()

    barrier = pltpu.get_barrier_semaphore()
    chips = chip_partners(tm, row, tm_n, rows_n)
    twin = (tm + 1 - 2 * lax.rem(tm, CORES), row)
    partners = chips + [(tm_at(d), row_at(e)) for e in (-1, 1, 0) for d in (-1, 1)]
    for p in partners:
        pl.semaphore_signal(barrier, inc=1, device_id=p, device_id_type=MESH)
    pl.semaphore_wait(barrier, len(partners))

    both = jnp.logical_and
    peers = [
        (next_ok, (tm_at(1), row)),
        (up_ok, (tm, row_at(-1))),
        (down_ok, (tm, row_at(1))),
        (both(next_ok, up_ok), (tm_at(1), row_at(-1))),
        (both(next_ok, down_ok), (tm_at(1), row_at(1))),
    ]
    arrives = [prev_ok, down_ok, up_ok, both(prev_ok, down_ok), both(prev_ok, up_ok)]

    def exchange(which, sources, targets):
        copies = []
        for n in range(5):
            ok, device = peers[n]
            copy = pltpu.make_async_remote_copy(
                src_ref=sources[n], dst_ref=targets[n],
                send_sem=hs_sem.at[which, n], recv_sem=hr_sem.at[which, n],
                device_id=device, device_id_type=MESH,
            )
            pl.when(ok)(copy.start)
            copies.append(copy)
        return copies

    def send(which, ref, n, device):
        pltpu.make_async_remote_copy(
            src_ref=ref.at[0], dst_ref=ref.at[n],
            send_sem=rs_sem.at[which], recv_sem=rr_sem.at[which],
            device_id=device, device_id_type=MESH,
        ).start()

    def arrived(which, ref):
        n = ref.shape[0]
        pltpu.make_async_copy(ref.at[1:n], ref.at[1:n], rr_sem.at[which]).wait()
        return jnp.sum(ref[...], axis=0)

    def reduce_chip(which, value):
        ref = red_core.at[which]
        ref[0] = value
        send(2 * which, ref, 1, twin)

    def reduce_all(which):
        ref = red_chip.at[which]
        ref[0] = arrived(2 * which, red_core.at[which])
        for n, device in enumerate(chips):
            send(2 * which + 1, ref, n + 1, device)

    def reduced(which):
        return arrived(2 * which + 1, red_chip.at[which])

    boxes = [(0, 2, 1, 3), (2, 4, 3, 4), (2, 4, 0, 1), (0, 2, 3, 4), (0, 2, 0, 1)]
    halo1 = exchange(
        0,
        [latent, latent.at[:, 0:1], latent.at[:, 1:2], latent.at[:, 0:1], latent.at[:, 1:2]],
        [lx.at[a:b, c:d] for a, b, c, d in boxes],
    )
    load.wait()
    x = lx[2:4, 1:3].astype(jnp.float32).reshape(frames * height * width, cin)
    reduce_chip(0, pack_stats(jnp.sum(x, axis=0, keepdims=True), jnp.sum(x * x, axis=0, keepdims=True)))
    reduce_all(0)
    for c in w2_loads:
        c.wait()

    def merge(i):
        for k in range(TAPS):
            mid = w2m[i, k].astype(jnp.float32)
            w2[0, k, slot[i] + 1] = (mid + w2[1, k, slot[i] + 1].astype(jnp.float32)).astype(jnp.bfloat16)
            w2[1, k, slot[i]] = (mid + w2[0, k, slot[i]].astype(jnp.float32)).astype(jnp.bfloat16)

    for i in range(TAPS):
        merge(i)
    for c in small:
        c.wait()
    count = tm_n * rows_n * frames * height * width * (cin // GROUPS)
    a, b = affine(reduced(0), count, g1[...], s1[...])

    def normalize(source, target, box, a, b):
        f0, f1, r0, r1 = box
        for f in range(f0, f1):
            for r in range(r0, r1):
                target[f, r] = activate(source[f, r], a, b)

    def normalize_halo(n, copy, source, target, box, a, b):
        f0, f1, r0, r1 = box

        @pl.when(arrives[n])
        def _():
            copy.wait_recv()
            normalize(source, target, box, a, b)

        @pl.when(jnp.logical_not(arrives[n]))
        def _():
            target[f0:f1, r0:r1] = jnp.zeros((f1 - f0, r1 - r0) + target.shape[2:], target.dtype)

    normalize(lx, xn, (2, 4, 1, 3), a, b)
    for n in range(5):
        normalize_halo(n, halo1[n], lx, xn, boxes[n], a, b)
    for c in w1_loads:
        c.wait()

    size = frames * height * width
    column = lax.rem(lax.broadcasted_iota(jnp.int32, (size, cout), 0), width)
    after = lambda y: jnp.where(column == 0, 0.0, pltpu.roll(y, 1, 0))
    before = lambda y: jnp.where(column == width - 1, 0.0, pltpu.roll(y, size - 1, 0))

    lhs = jnp.concatenate(
        [xn[i : i + frames, j : j + height].reshape(size, cin) for i in range(TAPS) for j in range(TAPS)], axis=1
    )
    y = [
        jnp.dot(lhs, w1[k].reshape(TAPS * TAPS * cin, cout), preferred_element_type=jnp.float32)
        for k in range(TAPS)
    ]
    middle = (after(y[0]) + y[1] + before(y[2])).astype(jnp.bfloat16)
    mx[1:3, 1:3] = middle.reshape(frames, height, width, cout)

    boxes = [(0, 1, 1, 3), (1, 3, 3, 4), (1, 3, 0, 1), (0, 1, 3, 4), (0, 1, 0, 1)]
    halo2 = exchange(
        1,
        [mx.at[2:3, 1:3], mx.at[1:3, 1:2], mx.at[1:3, 2:3], mx.at[2:3, 1:2], mx.at[2:3, 2:3]],
        [mx.at[a:b, c:d] for a, b, c, d in boxes],
    )
    x = middle.astype(jnp.float32)
    reduce_chip(1, pack_stats(jnp.sum(x, axis=0, keepdims=True), jnp.sum(x * x, axis=0, keepdims=True)))
    reduce_all(1)
    count = tm_n * rows_n * frames * height * width * (cout // GROUPS)
    a, b = affine(reduced(1), count, g2[...], s2[...])
    normalize(mx, sn, (1, 3, 1, 3), a, b)
    for n in range(5):
        normalize_halo(n, halo2[n], mx, sn, boxes[n], a, b)

    writes = []
    for rb in range(2):
        near = [sn[f : f + 2, r : r + height].reshape(size, cout) for f in (0, 1) for r in (rb, rb + 1)]
        lhs_s = jnp.concatenate(near, axis=1)
        far = [sn[0:3, r : r + height].reshape(3 * height * width, cout) for r in (rb, rb + 1)]
        lhs_r = jnp.concatenate(far, axis=1)
        s = [
            jnp.dot(lhs_s, w2[rb, k, 0:4].reshape(4 * cout, cout), preferred_element_type=jnp.float32)
            for k in range(TAPS)
        ]
        q = [
            jnp.dot(lhs_r, w2[rb, k, 4:6].reshape(2 * cout, cout), preferred_element_type=jnp.float32)
            for k in range(TAPS)
        ]
        for ta in range(2):
            skip = ta * height * width
            z = [s[k] + q[k][skip : skip + size] for k in range(TAPS)]
            pair = (after(z[0]) + z[1] + z[2], z[0] + z[1] + before(z[2]))
            for n in range(cout // LANES):
                part = slice(n * LANES, (n + 1) * LANES)
                for tc in range(2):
                    stage[n, pl.ds(tc, size, stride=2), :] = pair[tc][:, part]
                ob[rb, ta, :, :, :, part] = stage[n].astype(jnp.bfloat16).reshape(frames, height, 2 * width, LANES)
            for t in range(frames):
                for h in range(height):
                    write = pltpu.make_async_copy(
                        ob.at[rb, ta, t, h], out.at[2 * t + ta, 2 * h + rb], out_sem.at[rb, ta, t, h]
                    )
                    write.start()
                    writes.append(write)

    for c in writes:
        c.wait()
    for copies in (halo1, halo2):
        for n in range(5):
            pl.when(peers[n][0])(copies[n].wait_send)
    for which in range(2):
        for ref, n in ((red_core, 2 * which), (red_chip, 2 * which + 1)):
            rest = ref.at[which, 1 : ref.shape[1]]
            pltpu.make_async_copy(rest, rest, rs_sem.at[n]).wait()


def solution(mesh):
    tm_n, rows_n = mesh.shape["tm"], mesh.shape["rows"]

    def per_device(latent, gain1, shift1, kernel1, gain2, shift2, kernel2):
        frames, height, width, cin = latent.shape
        cout = kernel1.shape[-1]
        bf16, f32 = jnp.bfloat16, jnp.float32
        dma = pltpu.SemaphoreType.DMA
        return pl.pallas_call(
            functools.partial(kernel, tm_n, rows_n),
            out_shape=jax.ShapeDtypeStruct((2 * frames, 2 * height, 2 * width, cout), bf16),
            in_specs=[pl.BlockSpec(memory_space=pltpu.HBM)] * 7,
            out_specs=pl.BlockSpec(memory_space=pltpu.HBM),
            scratch_shapes=[
                pltpu.VMEM((frames + 2, height + 2, width, cin), bf16),
                pltpu.VMEM((frames + 2, height + 2, width, cin), bf16),
                pltpu.VMEM((TAPS, TAPS, TAPS, cin, cout), bf16),
                pltpu.VMEM((2, TAPS, 6, cout, cout), bf16),
                pltpu.VMEM((TAPS, TAPS, cout, cout), bf16),
                pltpu.VMEM((frames + 1, height + 2, width, cout), bf16),
                pltpu.VMEM((frames + 1, height + 2, width, cout), bf16),
                pltpu.VMEM((cout // LANES, 2 * frames * height * width, LANES), f32),
                pltpu.VMEM((2, 2, frames, height, 2 * width, cout), bf16),
                pltpu.VMEM((1, cin), f32),
                pltpu.VMEM((1, cin), f32),
                pltpu.VMEM((1, cout), f32),
                pltpu.VMEM((1, cout), f32),
                pltpu.VMEM((2, CORES, 1, LANES), f32),
                pltpu.VMEM((2, tm_n * rows_n // CORES, 1, LANES), f32),
                dma((5,)),
                dma((TAPS * TAPS,)),
                dma((TAPS * TAPS,)),
                dma((2, 2, frames, height)),
                dma((2, 5)),
                dma((2, 5)),
                dma((4,)),
                dma((4,)),
            ],
            compiler_params=pltpu.CompilerParams(
                collective_id=0, has_side_effects=True, vmem_limit_bytes=63 * 1024 * 1024
            ),
        )(
            latent, gain1.reshape(1, -1), shift1.reshape(1, -1), kernel1,
            gain2.reshape(1, -1), shift2.reshape(1, -1), kernel2,
        )

    placed = (P("tm", "rows", None, None), P(), P(), P(), P(), P(), P())
    return jax.shard_map(
        per_device, mesh=mesh, in_specs=placed, out_specs=P("tm", "rows", None, None), check_vma=False
    )
```

```python
import functools

import jax
import jax.numpy as jnp
from jax import lax
from jax.experimental import pallas as pl
from jax.experimental.pallas import tpu as pltpu
from jax.sharding import PartitionSpec as P

GROUPS = 32
EPS = 1e-06
MESH = pl.DeviceIdType.MESH
LANES = 128
TAPS = 3
CORES = 2
SIDE = 4


def chip_partners(tm, row, tm_n, rows_n):
    at_z = [lax.rem(tm + CORES * d, tm_n) for d in range(tm_n // CORES)]
    at_y = [lax.rem(row - lax.rem(row, SIDE) + SIDE * d, rows_n) for d in range(rows_n // SIDE)]
    at_x = [lax.rem(row + d, SIDE) for d in range(SIDE)]
    hops = lambda d, n: min(d, n - d)
    steps = [
        (-hops(dz, len(at_z)) - hops(dy, len(at_y)) - hops(dx, SIDE), dz, dy, dx)
        for dz in range(len(at_z))
        for dy in range(len(at_y))
        for dx in range(SIDE)
        if dz or dy or dx
    ]
    return [(at_z[dz], at_y[dy] + at_x[dx]) for _, dz, dy, dx in sorted(steps)]


def lane_sums(x, size):
    lane = lax.broadcasted_iota(jnp.int32, x.shape, 1)
    d = 1
    while d < size:
        other = jnp.where((lane & d) == 0, pltpu.roll(x, LANES - d, 1), pltpu.roll(x, d, 1))
        x = x + other
        d *= 2
    return x


def diagonal(size):
    lane = lax.broadcasted_iota(jnp.int32, (8, LANES), 1)
    sub = lax.broadcasted_iota(jnp.int32, (8, LANES), 0)
    return (lane & (size - 1)) == sub


def pack_stats(total, square):
    blocks = total.shape[1] // LANES
    size = total.shape[1] // GROUPS
    sub = lax.broadcasted_iota(jnp.int32, (8, LANES), 0)
    rows = jnp.zeros((8, LANES), jnp.float32)
    for v in range(blocks):
        part = slice(v * LANES, (v + 1) * LANES)
        rows = jnp.where(sub == v, total[:, part], rows)
        rows = jnp.where(sub == blocks + v, square[:, part], rows)
    rows = lane_sums(rows, size)
    return jnp.sum(jnp.where(diagonal(size), rows, 0.0), axis=0, keepdims=True)


def affine(packed, count, gain, shift):
    chans = gain.shape[1]
    blocks, size = chans // LANES, chans // GROUPS
    rows = jnp.where(diagonal(size), jnp.broadcast_to(packed, (8, LANES)), 0.0)
    rows = lane_sums(rows, size) * (1.0 / count)
    mean = rows
    spread = pltpu.roll(rows, 8 - blocks, 0) - mean * mean
    scale = lax.rsqrt(spread + EPS) * 0.5
    a = jnp.concatenate([scale[v : v + 1] for v in range(blocks)], axis=1) * gain
    m = jnp.concatenate([mean[v : v + 1] for v in range(blocks)], axis=1)
    return a, shift * 0.5 - m * a


def activate(x, a, b):
    half = x.astype(jnp.float32) * a + b
    return (half + half * jnp.tanh(half)).astype(jnp.bfloat16)


def kernel(
    tm_n, rows_n,
    latent, gain1, shift1, kernel1, gain2, shift2, kernel2, out,
    lx, xn, w1, w2, w2m, mx, sn, stage, g1, s1, g2, s2, red_core, red_chip,
    load_sem, w1_sem, w2_sem, hs_sem, hr_sem, rs_sem, rr_sem,
):
    tm, row = lax.axis_index("tm"), lax.axis_index("rows")
    frames, height, width, cin = latent.shape
    cout = kernel1.shape[-1]
    up_ok, down_ok = row > 0, row < rows_n - 1
    prev_ok, next_ok = tm > 0, tm < tm_n - 1
    tm_at = lambda d: lax.rem(tm + d + tm_n, tm_n)
    row_at = lambda d: lax.rem(row + d + rows_n, rows_n)

    own = lx.at[2:4, 1:3]
    load = pltpu.make_async_copy(latent, own, load_sem.at[0])
    load.start()
    small = [
        pltpu.make_async_copy(src, dst, load_sem.at[1 + n])
        for n, (src, dst) in enumerate(((gain1, g1), (shift1, s1), (gain2, g2), (shift2, s2)))
    ]
    for c in small:
        c.start()
    slot = (0, 4, 2)
    w2_loads, w1_loads = [], []
    for i in range(TAPS):
        w2_loads.append(pltpu.make_async_copy(kernel2.at[i, 0], w2.at[0, :, slot[i]], w2_sem.at[3 * i]))
        w2_loads.append(pltpu.make_async_copy(kernel2.at[i, 1], w2m.at[i], w2_sem.at[3 * i + 1]))
        w2_loads.append(pltpu.make_async_copy(kernel2.at[i, 2], w2.at[1, :, slot[i] + 1], w2_sem.at[3 * i + 2]))
    for i in range(TAPS):
        for k in range(TAPS):
            w1_loads.append(pltpu.make_async_copy(kernel1.at[i, :, k], w1.at[k, i], w1_sem.at[TAPS * i + k]))
    for c in w2_loads + w1_loads:
        c.start()

    barrier = pltpu.get_barrier_semaphore()
    chips = chip_partners(tm, row, tm_n, rows_n)
    twin = (tm + 1 - 2 * lax.rem(tm, CORES), row)
    partners = chips + [(tm_at(d), row_at(e)) for e in (-1, 1, 0) for d in (-1, 1)]
    for p in partners:
        pl.semaphore_signal(barrier, inc=1, device_id=p, device_id_type=MESH)
    load.wait()
    x = lx[2:4, 1:3].astype(jnp.float32).reshape(frames * height * width, cin)
    red_core[0, 0] = pack_stats(jnp.sum(x, axis=0, keepdims=True), jnp.sum(x * x, axis=0, keepdims=True))
    pl.semaphore_wait(barrier, len(partners))

    both = jnp.logical_and
    peers = [
        (next_ok, (tm_at(1), row)),
        (up_ok, (tm, row_at(-1))),
        (down_ok, (tm, row_at(1))),
        (both(next_ok, up_ok), (tm_at(1), row_at(-1))),
        (both(next_ok, down_ok), (tm_at(1), row_at(1))),
    ]
    first_core = lax.rem(tm, CORES) == 0
    arrives = [prev_ok, down_ok, up_ok, both(prev_ok, down_ok), both(prev_ok, up_ok)]

    def exchange(which, sources, targets):
        copies = []
        for n in range(5):
            device = peers[n][1]
            copy = pltpu.make_async_remote_copy(
                src_ref=sources[n], dst_ref=targets[n],
                send_sem=hs_sem.at[which, n], recv_sem=hr_sem.at[which, n],
                device_id=device, device_id_type=MESH,
            )
            copies.append(copy)
        return copies

    def goes(copies, n):
        return both(peers[n][0], jnp.logical_not(first_core)) if copies is halo1 and n >= 3 else peers[n][0]

    def start(copies, which):
        for n in which:
            pl.when(goes(copies, n))(copies[n].start)

    def send(which, ref, n, device):
        pltpu.make_async_remote_copy(
            src_ref=ref.at[0], dst_ref=ref.at[n],
            send_sem=rs_sem.at[which], recv_sem=rr_sem.at[which],
            device_id=device, device_id_type=MESH,
        ).start()

    def arrived(which, ref):
        n = ref.shape[0]
        pltpu.make_async_copy(ref.at[1:n], ref.at[1:n], rr_sem.at[which]).wait()
        return jnp.sum(ref[...], axis=0)

    def reduce_chip(which):
        send(2 * which, red_core.at[which], 1, twin)

    def reduce_all(which):
        ref = red_chip.at[which]
        ref[0] = arrived(2 * which, red_core.at[which])
        for n, device in enumerate(chips):
            send(2 * which + 1, ref, n + 1, device)

    def reduced(which):
        return arrived(2 * which + 1, red_chip.at[which])

    boxes = [(0, 2, 1, 3), (2, 4, 3, 4), (2, 4, 0, 1), (0, 2, 3, 4), (0, 2, 0, 1)]
    halo1 = exchange(
        0,
        [latent, latent.at[:, 0:1], latent.at[:, 1:2], latent.at[:, 0:1], latent.at[:, 1:2]],
        [lx.at[a:b, c:d] for a, b, c, d in boxes],
    )
    reduce_chip(0)
    reduce_all(0)
    start(halo1, (1, 2, 3, 4, 0))
    for c in w2_loads:
        c.wait()

    def merge(i):
        for k in range(TAPS):
            mid = w2m[i, k].astype(jnp.float32)
            w2[0, k, slot[i] + 1] = (mid + w2[1, k, slot[i] + 1].astype(jnp.float32)).astype(jnp.bfloat16)
            w2[1, k, slot[i]] = (mid + w2[0, k, slot[i]].astype(jnp.float32)).astype(jnp.bfloat16)

    for i in range(TAPS):
        merge(i)
    forward = []
    for n in (1, 2):
        f0, f1, r0, r1 = boxes[n]
        copy = pltpu.make_async_remote_copy(
            src_ref=lx.at[f0:f1, r0:r1], dst_ref=lx.at[0:2, r0:r1],
            send_sem=hs_sem.at[0, n + 2], recv_sem=hr_sem.at[0, n + 2],
            device_id=twin, device_id_type=MESH,
        )
        pl.when(arrives[n])(halo1[n].wait_recv)
        pl.when(both(arrives[n], first_core))(copy.start)
        forward.append(copy)
    for c in small:
        c.wait()
    count = tm_n * rows_n * frames * height * width * (cin // GROUPS)
    a, b = affine(reduced(0), count, g1[...], s1[...])

    def normalize(source, target, box, a, b):
        f0, f1, r0, r1 = box
        for f in range(f0, f1):
            for r in range(r0, r1):
                target[f, r] = activate(source[f, r], a, b)

    def normalize_halo(n, copy, source, target, box, a, b):
        f0, f1, r0, r1 = box

        @pl.when(arrives[n])
        def _():
            if copy is not halo1[1] and copy is not halo1[2]:
                copy.wait_recv()
            normalize(source, target, box, a, b)

        @pl.when(jnp.logical_not(arrives[n]))
        def _():
            target[f0:f1, r0:r1] = jnp.zeros((f1 - f0, r1 - r0) + target.shape[2:], target.dtype)

    normalize(lx, xn, (2, 4, 1, 3), a, b)
    for n in range(5):
        normalize_halo(n, halo1[n], lx, xn, boxes[n], a, b)
    for c in w1_loads:
        c.wait()

    size = frames * height * width
    column = lax.rem(lax.broadcasted_iota(jnp.int32, (size, cout), 0), width)
    after = lambda y: jnp.where(column == 0, 0.0, pltpu.roll(y, 1, 0))
    before = lambda y: jnp.where(column == width - 1, 0.0, pltpu.roll(y, size - 1, 0))

    lhs = jnp.concatenate(
        [xn[i : i + frames, j : j + height].reshape(size, cin) for i in range(TAPS) for j in range(TAPS)], axis=1
    )
    y = [
        jnp.dot(lhs, w1[k].reshape(TAPS * TAPS * cin, cout), preferred_element_type=jnp.float32)
        for k in range(TAPS)
    ]
    middle = (after(y[0]) + y[1] + before(y[2])).astype(jnp.bfloat16)
    mx[1:3, 1:3] = middle.reshape(frames, height, width, cout)

    boxes = [(0, 1, 1, 3), (1, 3, 3, 4), (1, 3, 0, 1), (0, 1, 3, 4), (0, 1, 0, 1)]
    halo2 = exchange(
        1,
        [mx.at[2:3, 1:3], mx.at[1:3, 1:2], mx.at[1:3, 2:3], mx.at[2:3, 1:2], mx.at[2:3, 2:3]],
        [mx.at[a:b, c:d] for a, b, c, d in boxes],
    )
    start(halo2, range(5))
    x = middle.astype(jnp.float32)
    red_core[1, 0] = pack_stats(jnp.sum(x, axis=0, keepdims=True), jnp.sum(x * x, axis=0, keepdims=True))
    reduce_chip(1)
    reduce_all(1)
    count = tm_n * rows_n * frames * height * width * (cout // GROUPS)
    a, b = affine(reduced(1), count, g2[...], s2[...])
    normalize(mx, sn, (1, 3, 1, 3), a, b)
    for n in range(5):
        normalize_halo(n, halo2[n], mx, sn, boxes[n], a, b)

    for rb in range(2):
        near = [sn[f : f + 2, r : r + height].reshape(size, cout) for f in (0, 1) for r in (rb, rb + 1)]
        lhs_s = jnp.concatenate(near, axis=1)
        far = [sn[0:3, r : r + height].reshape(3 * height * width, cout) for r in (rb, rb + 1)]
        lhs_r = jnp.concatenate(far, axis=1)
        s = [
            jnp.dot(lhs_s, w2[rb, k, 0:4].reshape(4 * cout, cout), preferred_element_type=jnp.float32)
            for k in range(TAPS)
        ]
        q = [
            jnp.dot(lhs_r, w2[rb, k, 4:6].reshape(2 * cout, cout), preferred_element_type=jnp.float32)
            for k in range(TAPS)
        ]
        for ta in range(2):
            skip = ta * height * width
            z = [s[k] + q[k][skip : skip + size] for k in range(TAPS)]
            pair = (after(z[0]) + z[1] + z[2], z[0] + z[1] + before(z[2]))
            for n in range(cout // LANES):
                part = slice(n * LANES, (n + 1) * LANES)
                for tc in range(2):
                    stage[n, pl.ds(tc, size, stride=2), :] = pair[tc][:, part]
                full = stage[n].astype(jnp.bfloat16).reshape(frames, height, 2 * width, LANES)
                for t in range(frames):
                    for h in range(height):
                        out[2 * t + ta, 2 * h + rb, :, part] = full[t, h]

    for copies in (halo1, halo2):
        for n in range(5):
            pl.when(goes(copies, n))(copies[n].wait_send)
    for n in (1, 2):
        pl.when(both(arrives[n], first_core))(forward[n - 1].wait_send)
    for which in range(2):
        for ref, n in ((red_core, 2 * which), (red_chip, 2 * which + 1)):
            rest = ref.at[which, 1 : ref.shape[1]]
            pltpu.make_async_copy(rest, rest, rs_sem.at[n]).wait()


def solution(mesh):
    tm_n, rows_n = mesh.shape["tm"], mesh.shape["rows"]

    def per_device(latent, gain1, shift1, kernel1, gain2, shift2, kernel2):
        frames, height, width, cin = latent.shape
        cout = kernel1.shape[-1]
        bf16, f32 = jnp.bfloat16, jnp.float32
        dma = pltpu.SemaphoreType.DMA
        return pl.pallas_call(
            functools.partial(kernel, tm_n, rows_n),
            out_shape=pltpu.VMEM((2 * frames, 2 * height, 2 * width, cout), bf16),
            in_specs=[pl.BlockSpec(memory_space=pltpu.HBM)] * 7,
            out_specs=pl.BlockSpec(memory_space=pltpu.VMEM),
            scratch_shapes=[
                pltpu.VMEM((frames + 2, height + 2, width, cin), bf16),
                pltpu.VMEM((frames + 2, height + 2, width, cin), bf16),
                pltpu.VMEM((TAPS, TAPS, TAPS, cin, cout), bf16),
                pltpu.VMEM((2, TAPS, 6, cout, cout), bf16),
                pltpu.VMEM((TAPS, TAPS, cout, cout), bf16),
                pltpu.VMEM((frames + 1, height + 2, width, cout), bf16),
                pltpu.VMEM((frames + 1, height + 2, width, cout), bf16),
                pltpu.VMEM((cout // LANES, 2 * frames * height * width, LANES), f32),
                pltpu.VMEM((1, cin), f32),
                pltpu.VMEM((1, cin), f32),
                pltpu.VMEM((1, cout), f32),
                pltpu.VMEM((1, cout), f32),
                pltpu.VMEM((2, CORES, 1, LANES), f32),
                pltpu.VMEM((2, tm_n * rows_n // CORES, 1, LANES), f32),
                dma((5,)),
                dma((TAPS * TAPS,)),
                dma((TAPS * TAPS,)),
                dma((2, 5)),
                dma((2, 5)),
                dma((4,)),
                dma((4,)),
            ],
            compiler_params=pltpu.CompilerParams(
                collective_id=0, has_side_effects=True, vmem_limit_bytes=48 * 1024 * 1024
            ),
        )(*(
            pltpu.with_memory_space_constraint(x, pltpu.HBM)
            for x in (
                latent, gain1.reshape(1, -1), shift1.reshape(1, -1), kernel1,
                gain2.reshape(1, -1), shift2.reshape(1, -1), kernel2,
            )
        ))

    placed = (P("tm", "rows", None, None), P(), P(), P(), P(), P(), P())
    return jax.shard_map(
        per_device, mesh=mesh, in_specs=placed, out_specs=P("tm", "rows", None, None), check_vma=False
    )
```

```python
import functools

import jax
import jax.numpy as jnp
from jax import lax
from jax.experimental import pallas as pl
from jax.experimental.pallas import tpu as pltpu
from jax.sharding import PartitionSpec as P

GROUPS = 32
EPS = 1e-06
MESH = pl.DeviceIdType.MESH
LANES = 128
TAPS = 3
CORES = 2
SIDE = 4


def partners_of(tm, row, tm_n, rows_n):
    z_n, y_n = tm_n // CORES, rows_n // SIDE
    core, x = lax.rem(tm, CORES), lax.rem(row, SIDE)
    y = lax.div(row, SIDE)
    at_z = [lax.rem(tm + CORES * d, tm_n) for d in range(z_n)]
    at_x = [lax.rem(x + d, SIDE) for d in range(SIDE)]
    pair = [y * SIDE, (y + 1 - 2 * lax.rem(y, 2)) * SIDE]
    mirror = [y * SIDE, (y_n - 1 - y) * SIDE]
    cores = [tm, tm + 1 - 2 * core]
    hops = lambda d, n: min(d, n - d)

    def ordered(places):
        return [device for _, _, device in sorted(places, key=lambda p: p[:2])[:-1]]

    near = ordered([
        (-hops(dx, SIDE) - dy, -n, (cores[n], pair[dy] + at_x[dx]))
        for dx in range(SIDE) for dy in range(2) for n in range(CORES)
    ])
    across = ordered([
        (-hops(dz, z_n) - dy, -dz, (at_z[dz], mirror[dy] + x)) for dz in range(z_n) for dy in range(2)
    ])
    return near, across


def thirds(x):
    high = x.astype(jnp.bfloat16).astype(jnp.float32)
    rest = x - high
    middle = rest.astype(jnp.bfloat16).astype(jnp.float32)
    return jnp.concatenate([high, middle, rest - middle, jnp.zeros_like(x)], axis=0).astype(jnp.bfloat16)


def member(shape, size, axis):
    chan = lax.broadcasted_iota(jnp.int32, shape, axis)
    group = lax.broadcasted_iota(jnp.int32, shape, 1 - axis)
    return (lax.div(chan, size) == group).astype(jnp.float32).astype(jnp.bfloat16)


def pack_stats(x, groups):
    parts = x.reshape(x.shape[0] // 8, 8, x.shape[1])
    sums = jnp.concatenate([jnp.sum(parts, axis=0), jnp.sum(parts * parts, axis=0)], axis=1)
    return jnp.sum(jnp.dot(thirds(sums), groups, preferred_element_type=jnp.float32), axis=0, keepdims=True)


def affine(packed, count, gain, shift, channels):
    chans = gain.shape[1]
    first = lax.broadcasted_iota(jnp.int32, (8, LANES), 0) == 0
    spread_out = jnp.dot(
        thirds(jnp.where(first, packed * (1.0 / count), 0.0)), channels, preferred_element_type=jnp.float32
    )
    moments = jnp.sum(spread_out, axis=0, keepdims=True)
    mean = moments[:, :chans]
    spread = moments[:, chans:] - mean * mean
    a = lax.rsqrt(spread + EPS) * 0.5 * gain
    return a, shift * 0.5 - mean * a


def activate(x, a, b):
    half = x.astype(jnp.float32) * a + b
    return (half + half * jnp.tanh(half)).astype(jnp.bfloat16)


def kernel(
    tm_n, rows_n,
    latent, gain1, shift1, kernel1, gain2, shift2, kernel2, out,
    lx, xn, w1, w2, w2m, mx, sn, stage, g1, s1, g2, s2, groups1, channels1, groups2, channels2, red_near, red_across, red_all,
    load_sem, w1_sem, w2_sem, hs_sem, hr_sem, rs_sem, rr_sem,
):
    tm, row = lax.axis_index("tm"), lax.axis_index("rows")
    frames, height, width, cin = latent.shape
    cout = kernel1.shape[-1]
    place = row * tm_n + tm
    up_ok, down_ok = row > 0, row < rows_n - 1
    prev_ok, next_ok = tm > 0, tm < tm_n - 1
    tm_at = lambda d: lax.rem(tm + d + tm_n, tm_n)
    row_at = lambda d: lax.rem(row + d + rows_n, rows_n)

    own = lx.at[2:4, 1:3]
    load = pltpu.make_async_copy(latent, own, load_sem.at[0])
    load.start()

    barrier = pltpu.get_barrier_semaphore()
    near, across = partners_of(tm, row, tm_n, rows_n)
    twin = (tm + 1 - 2 * lax.rem(tm, CORES), row)
    partners = [(tm_at(d), row_at(e)) for e in (-1, 1, 0) for d in (-1, 1)]
    partners = near + across + partners + [(tm, row_at(e)) for e in (-1, 1)]
    for p in partners:
        pl.semaphore_signal(barrier, inc=1, device_id=p, device_id_type=MESH)
    small = [
        pltpu.make_async_copy(src, dst, load_sem.at[1 + n])
        for n, (src, dst) in enumerate(((gain1, g1), (shift1, s1), (gain2, g2), (shift2, s2)))
    ]
    for c in small:
        c.start()
    slot = (0, 4, 2)
    w2_loads, w1_loads = [], []
    for i in range(TAPS):
        w2_loads.append(pltpu.make_async_copy(kernel2.at[i, 0], w2.at[0, :, slot[i]], w2_sem.at[3 * i]))
        w2_loads.append(pltpu.make_async_copy(kernel2.at[i, 1], w2m.at[i], w2_sem.at[3 * i + 1]))
        w2_loads.append(pltpu.make_async_copy(kernel2.at[i, 2], w2.at[1, :, slot[i] + 1], w2_sem.at[3 * i + 2]))
    for i in range(TAPS):
        for k in range(TAPS):
            w1_loads.append(pltpu.make_async_copy(kernel1.at[i, :, k], w1.at[k, i], w1_sem.at[TAPS * i + k]))
    for c in w2_loads + w1_loads:
        c.start()
    load.wait()
    x = lx[2:4, 1:3].astype(jnp.float32).reshape(frames * height * width, cin)
    groups1[...] = member(groups1.shape, cin // GROUPS, 0)
    red_near[0] = pack_stats(x, groups1[...])
    pl.semaphore_wait(barrier, len(partners))

    both = jnp.logical_and
    peers = [
        (next_ok, (tm_at(1), row)),
        (up_ok, (tm, row_at(-1))),
        (down_ok, (tm, row_at(1))),
        (both(next_ok, up_ok), (tm_at(1), row_at(-1))),
        (both(next_ok, down_ok), (tm_at(1), row_at(1))),
    ]
    first_core = lax.rem(tm, CORES) == 0
    arrives = [prev_ok, down_ok, up_ok, both(prev_ok, down_ok), both(prev_ok, up_ok)]

    def exchange(which, sources, targets):
        copies = []
        for n in range(5):
            device = peers[n][1]
            copy = pltpu.make_async_remote_copy(
                src_ref=sources[n], dst_ref=targets[n],
                send_sem=hs_sem.at[which, n], recv_sem=hr_sem.at[which, n],
                device_id=device, device_id_type=MESH,
            )
            copies.append(copy)
        return copies

    def goes(copies, n):
        return both(peers[n][0], jnp.logical_not(first_core)) if copies is halo1 and n >= 3 else peers[n][0]

    def start(copies, which):
        for n in which:
            pl.when(goes(copies, n))(copies[n].start)

    def send(which, ref, n, device):
        pltpu.make_async_remote_copy(
            src_ref=ref.at[0], dst_ref=ref.at[n],
            send_sem=rs_sem.at[which], recv_sem=rr_sem.at[which],
            device_id=device, device_id_type=MESH,
        ).start()

    def arrived(which, ref):
        n = ref.shape[0]
        pltpu.make_async_copy(ref.at[1:n], ref.at[1:n], rr_sem.at[which]).wait()
        return jnp.sum(ref[...], axis=0)

    def send_all(which, ref, devices):
        for n, device in enumerate(devices):
            send(which, ref, n + 1, device)

    boxes = [(0, 2, 1, 3), (2, 4, 3, 4), (2, 4, 0, 1), (0, 2, 3, 4), (0, 2, 0, 1)]
    halo1 = exchange(
        0,
        [latent, latent.at[:, 0:1], latent.at[:, 1:2], latent.at[:, 0:1], latent.at[:, 1:2]],
        [lx.at[a:b, c:d] for a, b, c, d in boxes],
    )
    send_all(0, red_near, near)
    start(halo1, (1, 2, 3, 4, 0))
    channels1[...] = member(channels1.shape, cin // GROUPS, 1)
    groups2[...] = member(groups2.shape, cout // GROUPS, 0)
    channels2[...] = member(channels2.shape, cout // GROUPS, 1)
    red_across[0] = arrived(0, red_near)
    send_all(1, red_across, across)
    for c in w2_loads:
        c.wait()

    def merge(i):
        for k in range(TAPS):
            mid = w2m[i, k].astype(jnp.float32)
            w2[0, k, slot[i] + 1] = (mid + w2[1, k, slot[i] + 1].astype(jnp.float32)).astype(jnp.bfloat16)
            w2[1, k, slot[i]] = (mid + w2[0, k, slot[i]].astype(jnp.float32)).astype(jnp.bfloat16)

    for i in range(TAPS):
        merge(i)
    forward = []
    for n in (1, 2):
        f0, f1, r0, r1 = boxes[n]
        copy = pltpu.make_async_remote_copy(
            src_ref=lx.at[f0:f1, r0:r1], dst_ref=lx.at[0:2, r0:r1],
            send_sem=hs_sem.at[0, n + 2], recv_sem=hr_sem.at[0, n + 2],
            device_id=twin, device_id_type=MESH,
        )
        pl.when(arrives[n])(halo1[n].wait_recv)
        pl.when(both(arrives[n], first_core))(copy.start)
        forward.append(copy)
    for c in small:
        c.wait()
    count = tm_n * rows_n * frames * height * width * (cin // GROUPS)
    a, b = affine(arrived(1, red_across), count, g1[...], s1[...], channels1[...])

    def normalize(source, target, box, a, b):
        f0, f1, r0, r1 = box
        for f in range(f0, f1):
            for r in range(r0, r1):
                target[f, r] = activate(source[f, r], a, b)

    def normalize_halo(n, copy, source, target, box, a, b):
        f0, f1, r0, r1 = box

        @pl.when(arrives[n])
        def _():
            if copy is not halo1[1] and copy is not halo1[2]:
                copy.wait_recv()
            normalize(source, target, box, a, b)

        @pl.when(jnp.logical_not(arrives[n]))
        def _():
            target[f0:f1, r0:r1] = jnp.zeros((f1 - f0, r1 - r0) + target.shape[2:], target.dtype)

    normalize(lx, xn, (2, 4, 1, 3), a, b)
    for n in range(5):
        normalize_halo(n, halo1[n], lx, xn, boxes[n], a, b)
    for c in w1_loads:
        c.wait()

    size = frames * height * width
    column = lax.rem(lax.broadcasted_iota(jnp.int32, (size, cout), 0), width)
    after = lambda y: jnp.where(column == 0, 0.0, pltpu.roll(y, 1, 0))
    before = lambda y: jnp.where(column == width - 1, 0.0, pltpu.roll(y, size - 1, 0))

    lhs = jnp.concatenate(
        [xn[i : i + frames, j : j + height].reshape(size, cin) for i in range(TAPS) for j in range(TAPS)], axis=1
    )
    y = [
        jnp.dot(lhs, w1[k].reshape(TAPS * TAPS * cin, cout), preferred_element_type=jnp.float32)
        for k in range(TAPS)
    ]
    middle = (after(y[0]) + y[1] + before(y[2])).astype(jnp.bfloat16)
    mx[1:3, 1:3] = middle.reshape(frames, height, width, cout)

    boxes = [(0, 1, 1, 3), (1, 3, 3, 4), (1, 3, 0, 1), (0, 1, 3, 4), (0, 1, 0, 1)]
    halo2 = exchange(
        1,
        [mx.at[2:3, 1:3], mx.at[1:3, 1:2], mx.at[1:3, 2:3], mx.at[2:3, 1:2], mx.at[2:3, 2:3]],
        [mx.at[a:b, c:d] for a, b, c, d in boxes],
    )
    x = middle.astype(jnp.float32)
    red_all[place] = pack_stats(x, groups2[...])
    @pl.loop(0, tm_n * rows_n - 1)
    def _(n):
        to = n + (place <= n).astype(jnp.int32)
        pltpu.make_async_remote_copy(
            src_ref=red_all.at[place], dst_ref=red_all.at[place],
            send_sem=rs_sem.at[2], recv_sem=rr_sem.at[2],
            device_id=(lax.rem(to, tm_n), lax.div(to, tm_n)), device_id_type=MESH,
        ).start()

    start(halo2, range(5))
    count = tm_n * rows_n * frames * height * width * (cout // GROUPS)
    a, b = affine(arrived(2, red_all), count, g2[...], s2[...], channels2[...])
    normalize(mx, sn, (1, 3, 1, 3), a, b)
    for n in range(5):
        normalize_halo(n, halo2[n], mx, sn, boxes[n], a, b)

    for rb in range(2):
        near = [sn[f : f + 2, r : r + height].reshape(size, cout) for f in (0, 1) for r in (rb, rb + 1)]
        lhs_s = jnp.concatenate(near, axis=1)
        far = [sn[0:3, r : r + height].reshape(3 * height * width, cout) for r in (rb, rb + 1)]
        lhs_r = jnp.concatenate(far, axis=1)
        s = [
            jnp.dot(lhs_s, w2[rb, k, 0:4].reshape(4 * cout, cout), preferred_element_type=jnp.float32)
            for k in range(TAPS)
        ]
        q = [
            jnp.dot(lhs_r, w2[rb, k, 4:6].reshape(2 * cout, cout), preferred_element_type=jnp.float32)
            for k in range(TAPS)
        ]
        for ta in range(2):
            skip = ta * height * width
            z = [s[k] + q[k][skip : skip + size] for k in range(TAPS)]
            pair = (after(z[0]) + z[1] + z[2], z[0] + z[1] + before(z[2]))
            for n in range(cout // LANES):
                part = slice(n * LANES, (n + 1) * LANES)
                for tc in range(2):
                    stage[rb, ta, n, pl.ds(tc, size, stride=2), :] = pair[tc][:, part]
                full = stage[rb, ta, n].astype(jnp.bfloat16).reshape(frames, height, 2 * width, LANES)
                for t in range(frames):
                    for h in range(height):
                        out[2 * t + ta, 2 * h + rb, :, part] = full[t, h]

    for copies in (halo1, halo2):
        for n in range(5):
            pl.when(goes(copies, n))(copies[n].wait_send)
    for n in (1, 2):
        pl.when(both(arrives[n], first_core))(forward[n - 1].wait_send)
    for which, ref in enumerate((red_near, red_across, red_all)):
        rest = ref.at[1 : ref.shape[0]]
        pltpu.make_async_copy(rest, rest, rs_sem.at[which]).wait()


def solution(mesh):
    tm_n, rows_n = mesh.shape["tm"], mesh.shape["rows"]

    def per_device(latent, gain1, shift1, kernel1, gain2, shift2, kernel2):
        frames, height, width, cin = latent.shape
        cout = kernel1.shape[-1]
        bf16, f32 = jnp.bfloat16, jnp.float32
        dma = pltpu.SemaphoreType.DMA
        return pl.pallas_call(
            functools.partial(kernel, tm_n, rows_n),
            out_shape=pltpu.VMEM((2 * frames, 2 * height, 2 * width, cout), bf16),
            in_specs=[pl.BlockSpec(memory_space=pltpu.HBM)] * 7,
            out_specs=pl.BlockSpec(memory_space=pltpu.VMEM),
            scratch_shapes=[
                pltpu.VMEM((frames + 2, height + 2, width, cin), bf16),
                pltpu.VMEM((frames + 2, height + 2, width, cin), bf16),
                pltpu.VMEM((TAPS, TAPS, TAPS, cin, cout), bf16),
                pltpu.VMEM((2, TAPS, 6, cout, cout), bf16),
                pltpu.VMEM((TAPS, TAPS, cout, cout), bf16),
                pltpu.VMEM((frames + 1, height + 2, width, cout), bf16),
                pltpu.VMEM((frames + 1, height + 2, width, cout), bf16),
                pltpu.VMEM((2, 2, cout // LANES, 2 * frames * height * width, LANES), f32),
                pltpu.VMEM((1, cin), f32),
                pltpu.VMEM((1, cin), f32),
                pltpu.VMEM((1, cout), f32),
                pltpu.VMEM((1, cout), f32),
                pltpu.VMEM((2 * cin, LANES), bf16),
                pltpu.VMEM((LANES, 2 * cin), bf16),
                pltpu.VMEM((2 * cout, LANES), bf16),
                pltpu.VMEM((LANES, 2 * cout), bf16),
                pltpu.VMEM((2 * SIDE * CORES, 1, LANES), f32),
                pltpu.VMEM((2 * tm_n // CORES, 1, LANES), f32),
                pltpu.VMEM((tm_n * rows_n, 1, LANES), f32),
                dma((5,)),
                dma((TAPS * TAPS,)),
                dma((TAPS * TAPS,)),
                dma((2, 5)),
                dma((2, 5)),
                dma((3,)),
                dma((3,)),
            ],
            compiler_params=pltpu.CompilerParams(
                collective_id=0, has_side_effects=True, vmem_limit_bytes=48 * 1024 * 1024
            ),
        )(*(
            pltpu.with_memory_space_constraint(x, pltpu.HBM)
            for x in (
                latent, gain1.reshape(1, -1), shift1.reshape(1, -1), kernel1,
                gain2.reshape(1, -1), shift2.reshape(1, -1), kernel2,
            )
        ))

    placed = (P("tm", "rows", None, None), P(), P(), P(), P(), P(), P())
    return jax.shard_map(
        per_device, mesh=mesh, in_specs=placed, out_specs=P("tm", "rows", None, None), check_vma=False
    )
```

```python
import functools

import jax
import jax.numpy as jnp
from jax import lax
from jax.experimental import pallas as pl
from jax.experimental.pallas import tpu as pltpu
from jax.sharding import PartitionSpec as P

GROUPS = 32
EPS = 1e-06
MESH = pl.DeviceIdType.MESH
LANES = 128
TAPS = 3
CORES = 2
SIDE = 4


def partners_of(tm, row, tm_n, rows_n):
    z_n, y_n = tm_n // CORES, rows_n // SIDE
    core, x = lax.rem(tm, CORES), lax.rem(row, SIDE)
    y = lax.div(row, SIDE)
    at_z = [lax.rem(tm + CORES * d, tm_n) for d in range(z_n)]
    at_x = [lax.rem(x + d, SIDE) for d in range(SIDE)]
    pair = [y * SIDE, (y + 1 - 2 * lax.rem(y, 2)) * SIDE]
    mirror = [y * SIDE, (y_n - 1 - y) * SIDE]
    cores = [tm, tm + 1 - 2 * core]
    hops = lambda d, n: min(d, n - d)

    def ordered(places):
        return [device for _, _, device in sorted(places, key=lambda p: p[:2])[:-1]]

    near = ordered([
        (-hops(dx, SIDE) - dy, -n, (cores[n], pair[dy] + at_x[dx]))
        for dx in range(SIDE) for dy in range(2) for n in range(CORES)
    ])
    across = ordered([
        (-hops(dz, z_n) - dy, -dz, (at_z[dz], mirror[dy] + x)) for dz in range(z_n) for dy in range(2)
    ])
    return near, across


def thirds(x):
    high = x.astype(jnp.bfloat16).astype(jnp.float32)
    rest = x - high
    middle = rest.astype(jnp.bfloat16).astype(jnp.float32)
    return jnp.concatenate([high, middle, rest - middle, jnp.zeros_like(x)], axis=0).astype(jnp.bfloat16)


def member(shape, size, axis):
    chan = lax.broadcasted_iota(jnp.int32, shape, axis)
    group = lax.broadcasted_iota(jnp.int32, shape, 1 - axis)
    return (lax.div(chan, size) == group).astype(jnp.float32).astype(jnp.bfloat16)


def pack_stats(x, groups):
    parts = x.reshape(x.shape[0] // 8, 8, x.shape[1])
    sums = jnp.concatenate([jnp.sum(parts, axis=0), jnp.sum(parts * parts, axis=0)], axis=1)
    return jnp.sum(jnp.dot(thirds(sums), groups, preferred_element_type=jnp.float32), axis=0, keepdims=True)


def affine(packed, count, gain, shift, channels):
    chans = gain.shape[1]
    first = lax.broadcasted_iota(jnp.int32, (8, LANES), 0) == 0
    spread_out = jnp.dot(
        thirds(jnp.where(first, packed * (1.0 / count), 0.0)), channels, preferred_element_type=jnp.float32
    )
    moments = jnp.sum(spread_out, axis=0, keepdims=True)
    mean = moments[:, :chans]
    spread = moments[:, chans:] - mean * mean
    a = lax.rsqrt(spread + EPS) * 0.5 * gain
    return a, shift * 0.5 - mean * a


def activate(x, a, b):
    half = x.astype(jnp.float32) * a + b
    return (half + half * jnp.tanh(half)).astype(jnp.bfloat16)


def kernel(
    tm_n, rows_n,
    latent, gain1, shift1, kernel1, gain2, shift2, kernel2, sn, w2,
    lx, xn, w1, w2m, mx, g1, s1, g2, s2, groups1, channels1, groups2, channels2, red_near, red_across, red_all,
    load_sem, w1_sem, w2_sem, hs_sem, hr_sem, rs_sem, rr_sem,
):
    tm, row = lax.axis_index("tm"), lax.axis_index("rows")
    frames, height, width, cin = latent.shape
    cout = kernel1.shape[-1]
    place = row * tm_n + tm
    up_ok, down_ok = row > 0, row < rows_n - 1
    prev_ok, next_ok = tm > 0, tm < tm_n - 1
    tm_at = lambda d: lax.rem(tm + d + tm_n, tm_n)
    row_at = lambda d: lax.rem(row + d + rows_n, rows_n)

    own = lx.at[2:4, 1:3]
    load = pltpu.make_async_copy(latent, own, load_sem.at[0])
    load.start()

    barrier = pltpu.get_barrier_semaphore()
    near, across = partners_of(tm, row, tm_n, rows_n)
    twin = (tm + 1 - 2 * lax.rem(tm, CORES), row)
    partners = [(tm_at(d), row_at(e)) for e in (-1, 1, 0) for d in (-1, 1)]
    partners = near + across + partners + [(tm, row_at(e)) for e in (-1, 1)]
    for p in partners:
        pl.semaphore_signal(barrier, inc=1, device_id=p, device_id_type=MESH)
    small = [
        pltpu.make_async_copy(src, dst, load_sem.at[1 + n])
        for n, (src, dst) in enumerate(((gain1, g1), (shift1, s1), (gain2, g2), (shift2, s2)))
    ]
    for c in small:
        c.start()
    slot = (0, 4, 2)
    w2_loads, w1_loads = [], []
    for i in range(TAPS):
        w2_loads.append(pltpu.make_async_copy(kernel2.at[i, 0], w2.at[0, :, slot[i]], w2_sem.at[3 * i]))
        w2_loads.append(pltpu.make_async_copy(kernel2.at[i, 1], w2m.at[i], w2_sem.at[3 * i + 1]))
        w2_loads.append(pltpu.make_async_copy(kernel2.at[i, 2], w2.at[1, :, slot[i] + 1], w2_sem.at[3 * i + 2]))
    for i in range(TAPS):
        for k in range(TAPS):
            w1_loads.append(pltpu.make_async_copy(kernel1.at[i, :, k], w1.at[k, i], w1_sem.at[TAPS * i + k]))
    for c in w2_loads + w1_loads:
        c.start()
    load.wait()
    x = lx[2:4, 1:3].astype(jnp.float32).reshape(frames * height * width, cin)
    groups1[...] = member(groups1.shape, cin // GROUPS, 0)
    red_near[0] = pack_stats(x, groups1[...])
    pl.semaphore_wait(barrier, len(partners))

    both = jnp.logical_and
    peers = [
        (next_ok, (tm_at(1), row)),
        (up_ok, (tm, row_at(-1))),
        (down_ok, (tm, row_at(1))),
        (both(next_ok, up_ok), (tm_at(1), row_at(-1))),
        (both(next_ok, down_ok), (tm_at(1), row_at(1))),
    ]
    first_core = lax.rem(tm, CORES) == 0
    arrives = [prev_ok, down_ok, up_ok, both(prev_ok, down_ok), both(prev_ok, up_ok)]

    def exchange(which, sources, targets):
        copies = []
        for n in range(5):
            device = peers[n][1]
            copy = pltpu.make_async_remote_copy(
                src_ref=sources[n], dst_ref=targets[n],
                send_sem=hs_sem.at[which, n], recv_sem=hr_sem.at[which, n],
                device_id=device, device_id_type=MESH,
            )
            copies.append(copy)
        return copies

    def goes(copies, n):
        return both(peers[n][0], jnp.logical_not(first_core)) if copies is halo1 and n >= 3 else peers[n][0]

    def start(copies, which):
        for n in which:
            pl.when(goes(copies, n))(copies[n].start)

    def send(which, ref, n, device):
        pltpu.make_async_remote_copy(
            src_ref=ref.at[0], dst_ref=ref.at[n],
            send_sem=rs_sem.at[which], recv_sem=rr_sem.at[which],
            device_id=device, device_id_type=MESH,
        ).start()

    def arrived(which, ref):
        n = ref.shape[0]
        pltpu.make_async_copy(ref.at[1:n], ref.at[1:n], rr_sem.at[which]).wait()
        return jnp.sum(ref[...], axis=0)

    def send_all(which, ref, devices):
        for n, device in enumerate(devices):
            send(which, ref, n + 1, device)

    boxes = [(0, 2, 1, 3), (2, 4, 3, 4), (2, 4, 0, 1), (0, 2, 3, 4), (0, 2, 0, 1)]
    halo1 = exchange(
        0,
        [latent, latent.at[:, 0:1], latent.at[:, 1:2], latent.at[:, 0:1], latent.at[:, 1:2]],
        [lx.at[a:b, c:d] for a, b, c, d in boxes],
    )
    send_all(0, red_near, near)
    start(halo1, (1, 2, 3, 4, 0))
    channels1[...] = member(channels1.shape, cin // GROUPS, 1)
    groups2[...] = member(groups2.shape, cout // GROUPS, 0)
    channels2[...] = member(channels2.shape, cout // GROUPS, 1)
    red_across[0] = arrived(0, red_near)
    send_all(1, red_across, across)
    for c in w2_loads:
        c.wait()

    def merge(i):
        for k in range(TAPS):
            mid = w2m[i, k].astype(jnp.float32)
            w2[0, k, slot[i] + 1] = (mid + w2[1, k, slot[i] + 1].astype(jnp.float32)).astype(jnp.bfloat16)
            w2[1, k, slot[i]] = (mid + w2[0, k, slot[i]].astype(jnp.float32)).astype(jnp.bfloat16)

    for i in range(TAPS):
        merge(i)
    forward = []
    for n in (1, 2):
        f0, f1, r0, r1 = boxes[n]
        copy = pltpu.make_async_remote_copy(
            src_ref=lx.at[f0:f1, r0:r1], dst_ref=lx.at[0:2, r0:r1],
            send_sem=hs_sem.at[0, n + 2], recv_sem=hr_sem.at[0, n + 2],
            device_id=twin, device_id_type=MESH,
        )
        pl.when(arrives[n])(halo1[n].wait_recv)
        pl.when(both(arrives[n], first_core))(copy.start)
        forward.append(copy)
    for c in small:
        c.wait()
    count = tm_n * rows_n * frames * height * width * (cin // GROUPS)
    a, b = affine(arrived(1, red_across), count, g1[...], s1[...], channels1[...])

    def normalize(source, target, box, a, b):
        f0, f1, r0, r1 = box
        for f in range(f0, f1):
            for r in range(r0, r1):
                target[f, r] = activate(source[f, r], a, b)

    def normalize_halo(n, copy, source, target, box, a, b):
        f0, f1, r0, r1 = box

        @pl.when(arrives[n])
        def _():
            if copy is not halo1[1] and copy is not halo1[2]:
                copy.wait_recv()
            normalize(source, target, box, a, b)

        @pl.when(jnp.logical_not(arrives[n]))
        def _():
            target[f0:f1, r0:r1] = jnp.zeros((f1 - f0, r1 - r0) + target.shape[2:], target.dtype)

    normalize(lx, xn, (2, 4, 1, 3), a, b)
    for n in range(5):
        normalize_halo(n, halo1[n], lx, xn, boxes[n], a, b)
    for c in w1_loads:
        c.wait()

    size = frames * height * width
    column = lax.rem(lax.broadcasted_iota(jnp.int32, (size, cout), 0), width)
    after = lambda y: jnp.where(column == 0, 0.0, pltpu.roll(y, 1, 0))
    before = lambda y: jnp.where(column == width - 1, 0.0, pltpu.roll(y, size - 1, 0))

    lhs = jnp.concatenate(
        [xn[i : i + frames, j : j + height].reshape(size, cin) for i in range(TAPS) for j in range(TAPS)], axis=1
    )
    y = [
        jnp.dot(lhs, w1[k].reshape(TAPS * TAPS * cin, cout), preferred_element_type=jnp.float32)
        for k in range(TAPS)
    ]
    middle = (after(y[0]) + y[1] + before(y[2])).astype(jnp.bfloat16)
    mx[1:3, 1:3] = middle.reshape(frames, height, width, cout)

    boxes = [(0, 1, 1, 3), (1, 3, 3, 4), (1, 3, 0, 1), (0, 1, 3, 4), (0, 1, 0, 1)]
    halo2 = exchange(
        1,
        [mx.at[2:3, 1:3], mx.at[1:3, 1:2], mx.at[1:3, 2:3], mx.at[2:3, 1:2], mx.at[2:3, 2:3]],
        [mx.at[a:b, c:d] for a, b, c, d in boxes],
    )
    x = middle.astype(jnp.float32)
    red_all[place] = pack_stats(x, groups2[...])
    @pl.loop(0, tm_n * rows_n - 1)
    def _(n):
        to = n + (place <= n).astype(jnp.int32)
        pltpu.make_async_remote_copy(
            src_ref=red_all.at[place], dst_ref=red_all.at[place],
            send_sem=rs_sem.at[2], recv_sem=rr_sem.at[2],
            device_id=(lax.rem(to, tm_n), lax.div(to, tm_n)), device_id_type=MESH,
        ).start()

    start(halo2, range(5))
    count = tm_n * rows_n * frames * height * width * (cout // GROUPS)
    a, b = affine(arrived(2, red_all), count, g2[...], s2[...], channels2[...])
    normalize(mx, sn, (1, 3, 1, 3), a, b)
    for n in range(5):
        normalize_halo(n, halo2[n], mx, sn, boxes[n], a, b)

    for copies in (halo1, halo2):
        for n in range(5):
            pl.when(goes(copies, n))(copies[n].wait_send)
    for n in (1, 2):
        pl.when(both(arrives[n], first_core))(forward[n - 1].wait_send)
    for which, ref in enumerate((red_near, red_across, red_all)):
        rest = ref.at[1 : ref.shape[0]]
        pltpu.make_async_copy(rest, rest, rs_sem.at[which]).wait()


def second_conv(sn, w2, out, stage, ob, out_sem):
    frames, height, width, cout = sn.shape[0] - 1, sn.shape[1] - 2, sn.shape[2], sn.shape[3]
    size = frames * height * width
    column = lax.rem(lax.broadcasted_iota(jnp.int32, (size, cout), 0), width)
    after = lambda y: jnp.where(column == 0, 0.0, pltpu.roll(y, 1, 0))
    before = lambda y: jnp.where(column == width - 1, 0.0, pltpu.roll(y, size - 1, 0))
    writes = []
    for rb in range(2):
        near = [sn[f : f + 2, r : r + height].reshape(size, cout) for f in (0, 1) for r in (rb, rb + 1)]
        lhs_s = jnp.concatenate(near, axis=1)
        far = [sn[0:3, r : r + height].reshape(3 * height * width, cout) for r in (rb, rb + 1)]
        lhs_r = jnp.concatenate(far, axis=1)
        s = [
            jnp.dot(lhs_s, w2[rb, k, 0:4].reshape(4 * cout, cout), preferred_element_type=jnp.float32)
            for k in range(TAPS)
        ]
        q = [
            jnp.dot(lhs_r, w2[rb, k, 4:6].reshape(2 * cout, cout), preferred_element_type=jnp.float32)
            for k in range(TAPS)
        ]
        for ta in range(2):
            skip = ta * height * width
            z = [s[k] + q[k][skip : skip + size] for k in range(TAPS)]
            pair = (after(z[0]) + z[1] + z[2], z[0] + z[1] + before(z[2]))
            for n in range(cout // LANES):
                part = slice(n * LANES, (n + 1) * LANES)
                for tc in range(2):
                    stage[rb, ta, n, pl.ds(tc, size, stride=2), :] = pair[tc][:, part]
                full = stage[rb, ta, n].astype(jnp.bfloat16).reshape(frames, height, 2 * width, LANES)
                ob[rb, ta, :, :, :, part] = full
            for t in range(frames):
                for h in range(height):
                    write = pltpu.make_async_copy(
                        ob.at[rb, ta, t, h], out.at[2 * t + ta, 2 * h + rb], out_sem.at[rb, ta, t, h]
                    )
                    write.start()
                    writes.append(write)
    for write in writes:
        write.wait()


def solution(mesh):
    tm_n, rows_n = mesh.shape["tm"], mesh.shape["rows"]

    def per_device(latent, gain1, shift1, kernel1, gain2, shift2, kernel2):
        frames, height, width, cin = latent.shape
        cout = kernel1.shape[-1]
        bf16, f32 = jnp.bfloat16, jnp.float32
        dma = pltpu.SemaphoreType.DMA
        padded, merged = pl.pallas_call(
            functools.partial(kernel, tm_n, rows_n),
            out_shape=(
                pltpu.VMEM((frames + 1, height + 2, width, cout), bf16),
                pltpu.VMEM((2, TAPS, 6, cout, cout), bf16),
            ),
            in_specs=[pl.BlockSpec(memory_space=pltpu.HBM)] * 7,
            out_specs=(pl.BlockSpec(memory_space=pltpu.VMEM),) * 2,
            scratch_shapes=[
                pltpu.VMEM((frames + 2, height + 2, width, cin), bf16),
                pltpu.VMEM((frames + 2, height + 2, width, cin), bf16),
                pltpu.VMEM((TAPS, TAPS, TAPS, cin, cout), bf16),
                pltpu.VMEM((TAPS, TAPS, cout, cout), bf16),
                pltpu.VMEM((frames + 1, height + 2, width, cout), bf16),
                pltpu.VMEM((1, cin), f32),
                pltpu.VMEM((1, cin), f32),
                pltpu.VMEM((1, cout), f32),
                pltpu.VMEM((1, cout), f32),
                pltpu.VMEM((2 * cin, LANES), bf16),
                pltpu.VMEM((LANES, 2 * cin), bf16),
                pltpu.VMEM((2 * cout, LANES), bf16),
                pltpu.VMEM((LANES, 2 * cout), bf16),
                pltpu.VMEM((2 * SIDE * CORES, 1, LANES), f32),
                pltpu.VMEM((2 * tm_n // CORES, 1, LANES), f32),
                pltpu.VMEM((tm_n * rows_n, 1, LANES), f32),
                dma((5,)),
                dma((TAPS * TAPS,)),
                dma((TAPS * TAPS,)),
                dma((2, 5)),
                dma((2, 5)),
                dma((3,)),
                dma((3,)),
            ],
            compiler_params=pltpu.CompilerParams(
                collective_id=0, has_side_effects=True, vmem_limit_bytes=48 * 1024 * 1024
            ),
        )(*(
            pltpu.with_memory_space_constraint(x, pltpu.HBM)
            for x in (
                latent, gain1.reshape(1, -1), shift1.reshape(1, -1), kernel1,
                gain2.reshape(1, -1), shift2.reshape(1, -1), kernel2,
            )
        ))
        return pl.pallas_call(
            second_conv,
            out_shape=pltpu.HBM((2 * frames, 2 * height, 2 * width, cout), bf16),
            in_specs=[pl.BlockSpec(memory_space=pltpu.VMEM)] * 2,
            out_specs=pl.BlockSpec(memory_space=pltpu.HBM),
            scratch_shapes=[
                pltpu.VMEM((2, 2, cout // LANES, 2 * frames * height * width, LANES), f32),
                pltpu.VMEM((2, 2, frames, height, 2 * width, cout), bf16),
                dma((2, 2, frames, height)),
            ],
            compiler_params=pltpu.CompilerParams(vmem_limit_bytes=32 * 1024 * 1024),
        )(padded, merged)

    placed = (P("tm", "rows", None, None), P(), P(), P(), P(), P(), P())
    return jax.shard_map(
        per_device, mesh=mesh, in_specs=placed, out_specs=P("tm", "rows", None, None), check_vma=False
    )
```

```python
import functools

import jax
import jax.numpy as jnp
from jax import lax
from jax.experimental import pallas as pl
from jax.experimental.pallas import tpu as pltpu
from jax.sharding import PartitionSpec as P

GROUPS = 32
EPS = 1e-06
MESH = pl.DeviceIdType.MESH
LANES = 128
TAPS = 3
CORES = 2
SIDE = 4


def partners_of(tm, row, tm_n, rows_n):
    z_n, y_n = tm_n // CORES, rows_n // SIDE
    core, x = lax.rem(tm, CORES), lax.rem(row, SIDE)
    y = lax.div(row, SIDE)
    at_z = [lax.rem(tm + CORES * d, tm_n) for d in range(z_n)]
    at_x = [lax.rem(x + d, SIDE) for d in range(SIDE)]
    pair = [y * SIDE, (y + 1 - 2 * lax.rem(y, 2)) * SIDE]
    mirror = [y * SIDE, (y_n - 1 - y) * SIDE]
    cores = [tm, tm + 1 - 2 * core]
    hops = lambda d, n: min(d, n - d)

    def ordered(places):
        return [device for _, _, device in sorted(places, key=lambda p: p[:2])[:-1]]

    near = ordered([
        (-hops(dx, SIDE) - dy, -n, (cores[n], pair[dy] + at_x[dx]))
        for dx in range(SIDE) for dy in range(2) for n in range(CORES)
    ])
    across = ordered([
        (-hops(dz, z_n) - dy, -dz, (at_z[dz], mirror[dy] + x)) for dz in range(z_n) for dy in range(2)
    ])
    return near, across


def thirds(x):
    high = x.astype(jnp.bfloat16).astype(jnp.float32)
    rest = x - high
    middle = rest.astype(jnp.bfloat16).astype(jnp.float32)
    return jnp.concatenate([high, middle, rest - middle, jnp.zeros_like(x)], axis=0).astype(jnp.bfloat16)


def member(shape, size, axis):
    chan = lax.broadcasted_iota(jnp.int32, shape, axis)
    group = lax.broadcasted_iota(jnp.int32, shape, 1 - axis)
    return (lax.div(chan, size) == group).astype(jnp.float32).astype(jnp.bfloat16)


def pack_stats(x, groups):
    parts = x.reshape(x.shape[0] // 8, 8, x.shape[1])
    sums = jnp.concatenate([jnp.sum(parts, axis=0), jnp.sum(parts * parts, axis=0)], axis=1)
    return jnp.sum(jnp.dot(thirds(sums), groups, preferred_element_type=jnp.float32), axis=0, keepdims=True)


def affine(packed, count, gain, shift, channels):
    chans = gain.shape[1]
    first = lax.broadcasted_iota(jnp.int32, (8, LANES), 0) == 0
    spread_out = jnp.dot(
        thirds(jnp.where(first, packed * (1.0 / count), 0.0)), channels, preferred_element_type=jnp.float32
    )
    moments = jnp.sum(spread_out, axis=0, keepdims=True)
    mean = moments[:, :chans]
    spread = moments[:, chans:] - mean * mean
    a = lax.rsqrt(spread + EPS) * 0.5 * gain
    return a, shift * 0.5 - mean * a


def activate(x, a, b):
    half = x.astype(jnp.float32) * a + b
    return (half + half * jnp.tanh(half)).astype(jnp.bfloat16)


def kernel(
    tm_n, rows_n,
    latent, gain1, shift1, kernel1, gain2, shift2, kernel2, sn, w2,
    lx, xn, w1, w2m, mx, g1, s1, g2, s2, groups1, channels1, groups2, channels2, red_near, red_across, red_all,
    load_sem, w1_sem, w2_sem, hs_sem, hr_sem, rs_sem, rr_sem,
):
    tm, row = lax.axis_index("tm"), lax.axis_index("rows")
    frames, height, width, cin = latent.shape
    cout = kernel1.shape[-1]
    place = row * tm_n + tm
    up_ok, down_ok = row > 0, row < rows_n - 1
    prev_ok, next_ok = tm > 0, tm < tm_n - 1
    tm_at = lambda d: lax.rem(tm + d + tm_n, tm_n)
    row_at = lambda d: lax.rem(row + d + rows_n, rows_n)

    own = lx.at[2:4, 1:3]
    load = pltpu.make_async_copy(latent, own, load_sem.at[0])
    load.start()

    barrier = pltpu.get_barrier_semaphore()
    near, across = partners_of(tm, row, tm_n, rows_n)
    twin = (tm + 1 - 2 * lax.rem(tm, CORES), row)
    partners = [(tm_at(d), row_at(e)) for e in (-1, 1, 0) for d in (-1, 1)]
    partners = (near + across + partners + [(tm, row_at(e)) for e in (-1, 1)])[::-1]
    for p in partners:
        pl.semaphore_signal(barrier, inc=1, device_id=p, device_id_type=MESH)
    small = [
        pltpu.make_async_copy(src, dst, load_sem.at[1 + n])
        for n, (src, dst) in enumerate(((gain1, g1), (shift1, s1), (gain2, g2), (shift2, s2)))
    ]
    for c in small:
        c.start()
    slot = (0, 4, 2)
    w2_loads, w1_loads = [], []
    for i in range(TAPS):
        w2_loads.append(pltpu.make_async_copy(kernel2.at[i, 0], w2.at[0, :, slot[i]], w2_sem.at[3 * i]))
        w2_loads.append(pltpu.make_async_copy(kernel2.at[i, 1], w2m.at[i], w2_sem.at[3 * i + 1]))
        w2_loads.append(pltpu.make_async_copy(kernel2.at[i, 2], w2.at[1, :, slot[i] + 1], w2_sem.at[3 * i + 2]))
    for i in range(TAPS):
        for k in range(TAPS):
            w1_loads.append(pltpu.make_async_copy(kernel1.at[i, :, k], w1.at[k, i], w1_sem.at[TAPS * i + k]))
    for c in w2_loads + w1_loads:
        c.start()
    load.wait()
    x = lx[2:4, 1:3].astype(jnp.float32).reshape(frames * height * width, cin)
    groups1[...] = member(groups1.shape, cin // GROUPS, 0)
    red_near[0] = pack_stats(x, groups1[...])
    pl.semaphore_wait(barrier, len(partners))

    both = jnp.logical_and
    peers = [
        (next_ok, (tm_at(1), row)),
        (up_ok, (tm, row_at(-1))),
        (down_ok, (tm, row_at(1))),
        (both(next_ok, up_ok), (tm_at(1), row_at(-1))),
        (both(next_ok, down_ok), (tm_at(1), row_at(1))),
    ]
    first_core = lax.rem(tm, CORES) == 0
    arrives = [prev_ok, down_ok, up_ok, both(prev_ok, down_ok), both(prev_ok, up_ok)]

    def exchange(which, sources, targets):
        copies = []
        for n in range(5):
            device = peers[n][1]
            copy = pltpu.make_async_remote_copy(
                src_ref=sources[n], dst_ref=targets[n],
                send_sem=hs_sem.at[which, n], recv_sem=hr_sem.at[which, n],
                device_id=device, device_id_type=MESH,
            )
            copies.append(copy)
        return copies

    def goes(copies, n):
        return both(peers[n][0], jnp.logical_not(first_core)) if copies is halo1 and n >= 3 else peers[n][0]

    def start(copies, which):
        for n in which:
            pl.when(goes(copies, n))(copies[n].start)

    def send(which, ref, n, device):
        pltpu.make_async_remote_copy(
            src_ref=ref.at[0], dst_ref=ref.at[n],
            send_sem=rs_sem.at[which], recv_sem=rr_sem.at[which],
            device_id=device, device_id_type=MESH,
        ).start()

    def arrived(which, ref):
        n = ref.shape[0]
        pltpu.make_async_copy(ref.at[1:n], ref.at[1:n], rr_sem.at[which]).wait()
        parts = ref[...]
        while n > 1:
            n //= 2
            parts = parts[:n] + parts[n:]
        return parts[0]

    def send_all(which, ref, devices):
        for n, device in enumerate(devices):
            send(which, ref, n + 1, device)

    boxes = [(0, 2, 1, 3), (2, 4, 3, 4), (2, 4, 0, 1), (0, 2, 3, 4), (0, 2, 0, 1)]
    halo1 = exchange(
        0,
        [latent, latent.at[:, 0:1], latent.at[:, 1:2], latent.at[:, 0:1], latent.at[:, 1:2]],
        [lx.at[a:b, c:d] for a, b, c, d in boxes],
    )
    send_all(0, red_near, near)
    start(halo1, (1, 2, 3, 4, 0))
    channels1[...] = member(channels1.shape, cin // GROUPS, 1)
    groups2[...] = member(groups2.shape, cout // GROUPS, 0)
    channels2[...] = member(channels2.shape, cout // GROUPS, 1)
    red_across[0] = arrived(0, red_near)
    send_all(1, red_across, across)
    for c in w2_loads:
        c.wait()

    def merge(i):
        for k in range(TAPS):
            mid = w2m[i, k].astype(jnp.float32)
            w2[0, k, slot[i] + 1] = (mid + w2[1, k, slot[i] + 1].astype(jnp.float32)).astype(jnp.bfloat16)
            w2[1, k, slot[i]] = (mid + w2[0, k, slot[i]].astype(jnp.float32)).astype(jnp.bfloat16)

    for i in range(TAPS):
        merge(i)
    forward = []
    for n in (1, 2):
        f0, f1, r0, r1 = boxes[n]
        copy = pltpu.make_async_remote_copy(
            src_ref=lx.at[f0:f1, r0:r1], dst_ref=lx.at[0:2, r0:r1],
            send_sem=hs_sem.at[0, n + 2], recv_sem=hr_sem.at[0, n + 2],
            device_id=twin, device_id_type=MESH,
        )
        pl.when(arrives[n])(halo1[n].wait_recv)
        pl.when(both(arrives[n], first_core))(copy.start)
        forward.append(copy)
    for c in small:
        c.wait()
    count = tm_n * rows_n * frames * height * width * (cin // GROUPS)
    a, b = affine(arrived(1, red_across), count, g1[...], s1[...], channels1[...])

    def normalize(source, target, box, a, b):
        f0, f1, r0, r1 = box
        for f in range(f0, f1):
            for r in range(r0, r1):
                target[f, r] = activate(source[f, r], a, b)

    def normalize_halo(n, copy, source, target, box, a, b):
        f0, f1, r0, r1 = box

        @pl.when(arrives[n])
        def _():
            if copy is not halo1[1] and copy is not halo1[2]:
                copy.wait_recv()
            normalize(source, target, box, a, b)

        @pl.when(jnp.logical_not(arrives[n]))
        def _():
            target[f0:f1, r0:r1] = jnp.zeros((f1 - f0, r1 - r0) + target.shape[2:], target.dtype)

    normalize(lx, xn, (2, 4, 1, 3), a, b)
    for n in range(5):
        normalize_halo(n, halo1[n], lx, xn, boxes[n], a, b)
    for c in w1_loads:
        c.wait()

    size = frames * height * width
    column = lax.rem(lax.broadcasted_iota(jnp.int32, (size, cout), 0), width)
    after = lambda y: jnp.where(column == 0, 0.0, pltpu.roll(y, 1, 0))
    before = lambda y: jnp.where(column == width - 1, 0.0, pltpu.roll(y, size - 1, 0))

    lhs = jnp.concatenate(
        [xn[i : i + frames, j : j + height].reshape(size, cin) for i in range(TAPS) for j in range(TAPS)], axis=1
    )
    y = [
        jnp.dot(lhs, w1[k].reshape(TAPS * TAPS * cin, cout), preferred_element_type=jnp.float32)
        for k in range(TAPS)
    ]
    middle = (after(y[0]) + y[1] + before(y[2])).astype(jnp.bfloat16)
    mx[1:3, 1:3] = middle.reshape(frames, height, width, cout)

    boxes = [(0, 1, 1, 3), (1, 3, 3, 4), (1, 3, 0, 1), (0, 1, 3, 4), (0, 1, 0, 1)]
    halo2 = exchange(
        1,
        [mx.at[2:3, 1:3], mx.at[1:3, 1:2], mx.at[1:3, 2:3], mx.at[2:3, 1:2], mx.at[2:3, 2:3]],
        [mx.at[a:b, c:d] for a, b, c, d in boxes],
    )
    x = middle.astype(jnp.float32)
    red_all[place] = pack_stats(x, groups2[...])
    @pl.loop(0, tm_n * rows_n - 1)
    def _(n):
        to = n + (place <= n).astype(jnp.int32)
        pltpu.make_async_remote_copy(
            src_ref=red_all.at[place], dst_ref=red_all.at[place],
            send_sem=rs_sem.at[2], recv_sem=rr_sem.at[2],
            device_id=(lax.rem(to, tm_n), lax.div(to, tm_n)), device_id_type=MESH,
        ).start()

    start(halo2, range(5))
    count = tm_n * rows_n * frames * height * width * (cout // GROUPS)
    a, b = affine(arrived(2, red_all), count, g2[...], s2[...], channels2[...])
    normalize(mx, sn, (1, 3, 1, 3), a, b)
    for n in range(5):
        normalize_halo(n, halo2[n], mx, sn, boxes[n], a, b)

    for copies in (halo1, halo2):
        for n in range(5):
            pl.when(goes(copies, n))(copies[n].wait_send)
    for n in (1, 2):
        pl.when(both(arrives[n], first_core))(forward[n - 1].wait_send)
    for which, ref in enumerate((red_near, red_across, red_all)):
        rest = ref.at[1 : ref.shape[0]]
        pltpu.make_async_copy(rest, rest, rs_sem.at[which]).wait()


def second_conv(sn, w2, out, stage, ob, out_sem):
    frames, height, width, cout = sn.shape[0] - 1, sn.shape[1] - 2, sn.shape[2], sn.shape[3]
    size = frames * height * width
    column = lax.rem(lax.broadcasted_iota(jnp.int32, (size, cout), 0), width)
    after = lambda y: jnp.where(column == 0, 0.0, pltpu.roll(y, 1, 0))
    before = lambda y: jnp.where(column == width - 1, 0.0, pltpu.roll(y, size - 1, 0))
    writes = []
    for rb in range(2):
        near = [sn[f : f + 2, r : r + height].reshape(size, cout) for f in (0, 1) for r in (rb, rb + 1)]
        lhs_s = jnp.concatenate(near, axis=1)
        far = [sn[0:3, r : r + height].reshape(3 * height * width, cout) for r in (rb, rb + 1)]
        lhs_r = jnp.concatenate(far, axis=1)
        s = [
            jnp.dot(lhs_s, w2[rb, k, 0:4].reshape(4 * cout, cout), preferred_element_type=jnp.float32)
            for k in range(TAPS)
        ]
        q = [
            jnp.dot(lhs_r, w2[rb, k, 4:6].reshape(2 * cout, cout), preferred_element_type=jnp.float32)
            for k in range(TAPS)
        ]
        for ta in range(2):
            skip = ta * height * width
            z = [s[k] + q[k][skip : skip + size] for k in range(TAPS)]
            pair = (after(z[0]) + z[1] + z[2], z[0] + z[1] + before(z[2]))
            for t in range(frames):
                for h in range(height):
                    place = (t * height + h) * width
                    for n in range(cout // LANES):
                        part = slice(n * LANES, (n + 1) * LANES)
                        for tc in range(2):
                            rows = pl.ds(2 * place + tc, width, stride=2)
                            stage[rb, ta, n, rows, :] = pair[tc][place : place + width, part]
                        full = stage[rb, ta, n, 2 * place : 2 * (place + width)]
                        ob[rb, ta, t, h, :, part] = full.astype(jnp.bfloat16)
                    write = pltpu.make_async_copy(
                        ob.at[rb, ta, t, h], out.at[2 * t + ta, 2 * h + rb], out_sem.at[rb, ta, t, h]
                    )
                    write.start()
                    writes.append(write)
    for write in writes:
        write.wait()


def solution(mesh):
    tm_n, rows_n = mesh.shape["tm"], mesh.shape["rows"]

    def per_device(latent, gain1, shift1, kernel1, gain2, shift2, kernel2):
        frames, height, width, cin = latent.shape
        cout = kernel1.shape[-1]
        bf16, f32 = jnp.bfloat16, jnp.float32
        dma = pltpu.SemaphoreType.DMA
        padded, merged = pl.pallas_call(
            functools.partial(kernel, tm_n, rows_n),
            out_shape=(
                pltpu.VMEM((frames + 1, height + 2, width, cout), bf16),
                pltpu.VMEM((2, TAPS, 6, cout, cout), bf16),
            ),
            in_specs=[pl.BlockSpec(memory_space=pltpu.HBM)] * 7,
            out_specs=(pl.BlockSpec(memory_space=pltpu.VMEM),) * 2,
            scratch_shapes=[
                pltpu.VMEM((frames + 2, height + 2, width, cin), bf16),
                pltpu.VMEM((frames + 2, height + 2, width, cin), bf16),
                pltpu.VMEM((TAPS, TAPS, TAPS, cin, cout), bf16),
                pltpu.VMEM((TAPS, TAPS, cout, cout), bf16),
                pltpu.VMEM((frames + 1, height + 2, width, cout), bf16),
                pltpu.VMEM((1, cin), f32),
                pltpu.VMEM((1, cin), f32),
                pltpu.VMEM((1, cout), f32),
                pltpu.VMEM((1, cout), f32),
                pltpu.VMEM((2 * cin, LANES), bf16),
                pltpu.VMEM((LANES, 2 * cin), bf16),
                pltpu.VMEM((2 * cout, LANES), bf16),
                pltpu.VMEM((LANES, 2 * cout), bf16),
                pltpu.VMEM((2 * SIDE * CORES, 1, LANES), f32),
                pltpu.VMEM((2 * tm_n // CORES, 1, LANES), f32),
                pltpu.VMEM((tm_n * rows_n, 1, LANES), f32),
                dma((5,)),
                dma((TAPS * TAPS,)),
                dma((TAPS * TAPS,)),
                dma((2, 5)),
                dma((2, 5)),
                dma((3,)),
                dma((3,)),
            ],
            compiler_params=pltpu.CompilerParams(
                collective_id=0, has_side_effects=True, vmem_limit_bytes=48 * 1024 * 1024
            ),
        )(*(
            pltpu.with_memory_space_constraint(x, pltpu.HBM)
            for x in (
                latent, gain1.reshape(1, -1), shift1.reshape(1, -1), kernel1,
                gain2.reshape(1, -1), shift2.reshape(1, -1), kernel2,
            )
        ))
        return pl.pallas_call(
            second_conv,
            out_shape=pltpu.HBM((2 * frames, 2 * height, 2 * width, cout), bf16),
            in_specs=[pl.BlockSpec(memory_space=pltpu.VMEM)] * 2,
            out_specs=pl.BlockSpec(memory_space=pltpu.HBM),
            scratch_shapes=[
                pltpu.VMEM((2, 2, cout // LANES, 2 * frames * height * width, LANES), f32),
                pltpu.VMEM((2, 2, frames, height, 2 * width, cout), bf16),
                dma((2, 2, frames, height)),
            ],
            compiler_params=pltpu.CompilerParams(vmem_limit_bytes=32 * 1024 * 1024),
        )(padded, merged)

    placed = (P("tm", "rows", None, None), P(), P(), P(), P(), P(), P())
    return jax.shard_map(
        per_device, mesh=mesh, in_specs=placed, out_specs=P("tm", "rows", None, None), check_vma=False
    )
```

```python
import functools

import jax
import jax.numpy as jnp
from jax import lax
from jax.experimental import pallas as pl
from jax.experimental.pallas import tpu as pltpu
from jax.sharding import PartitionSpec as P

GROUPS = 32
EPS = 1e-06
MESH = pl.DeviceIdType.MESH
LANES = 128
TAPS = 3
CORES = 2
SIDE = 4


def partners_of(tm, row, tm_n, rows_n):
    z_n, y_n = tm_n // CORES, rows_n // SIDE
    core, x = lax.rem(tm, CORES), lax.rem(row, SIDE)
    y = lax.div(row, SIDE)
    at_z = [lax.rem(tm + CORES * d, tm_n) for d in range(z_n)]
    at_x = [lax.rem(x + d, SIDE) for d in range(SIDE)]
    pair = [y * SIDE, (y + 1 - 2 * lax.rem(y, 2)) * SIDE]
    mirror = [y * SIDE, (y_n - 1 - y) * SIDE]
    cores = [tm, tm + 1 - 2 * core]
    hops = lambda d, n: min(d, n - d)

    def ordered(places):
        return [device for _, _, device in sorted(places, key=lambda p: p[:2])[:-1]]

    near = ordered([
        (-hops(dx, SIDE) - dy, -n, (cores[n], pair[dy] + at_x[dx]))
        for dx in range(SIDE) for dy in range(2) for n in range(CORES)
    ])
    across = ordered([
        (-hops(dz, z_n) - dy, -dz, (at_z[dz], mirror[dy] + x)) for dz in range(z_n) for dy in range(2)
    ])
    return near, across


def thirds(x):
    high = x.astype(jnp.bfloat16).astype(jnp.float32)
    rest = x - high
    middle = rest.astype(jnp.bfloat16).astype(jnp.float32)
    return jnp.concatenate([high, middle, rest - middle, jnp.zeros_like(x)], axis=0).astype(jnp.bfloat16)


def member(shape, size, axis):
    chan = lax.broadcasted_iota(jnp.int32, shape, axis)
    group = lax.broadcasted_iota(jnp.int32, shape, 1 - axis)
    return (lax.div(chan, size) == group).astype(jnp.float32).astype(jnp.bfloat16)


def pack_stats(x, groups):
    parts = x.reshape(x.shape[0] // 8, 8, x.shape[1])
    sums = jnp.concatenate([jnp.sum(parts, axis=0), jnp.sum(parts * parts, axis=0)], axis=1)
    return jnp.sum(jnp.dot(thirds(sums), groups, preferred_element_type=jnp.float32), axis=0, keepdims=True)


def affine(packed, count, gain, shift, channels):
    chans = gain.shape[1]
    first = lax.broadcasted_iota(jnp.int32, (8, LANES), 0) == 0
    spread_out = jnp.dot(
        thirds(jnp.where(first, packed * (1.0 / count), 0.0)), channels, preferred_element_type=jnp.float32
    )
    moments = jnp.sum(spread_out, axis=0, keepdims=True)
    mean = moments[:, :chans]
    spread = moments[:, chans:] - mean * mean
    a = lax.rsqrt(spread + EPS) * 0.5 * gain
    return a, shift * 0.5 - mean * a


def activate(x, a, b):
    half = x.astype(jnp.float32) * a + b
    return (half + half * jnp.tanh(half)).astype(jnp.bfloat16)


def kernel(
    tm_n, rows_n,
    latent, gain1, shift1, kernel1, gain2, shift2, kernel2, sn, w2,
    lx, xn, w1, w2m, mx, g1, s1, g2, s2, groups1, channels1, groups2, channels2, red_near, red_across, red_all,
    load_sem, w1_sem, w2_sem, hs_sem, hr_sem, rs_sem, rr_sem,
):
    tm, row = lax.axis_index("tm"), lax.axis_index("rows")
    frames, height, width, cin = latent.shape
    cout = kernel1.shape[-1]
    place = row * tm_n + tm
    up_ok, down_ok = row > 0, row < rows_n - 1
    prev_ok, next_ok = tm > 0, tm < tm_n - 1
    tm_at = lambda d: lax.rem(tm + d + tm_n, tm_n)
    row_at = lambda d: lax.rem(row + d + rows_n, rows_n)

    own = lx.at[2:4, 1:3]
    load = pltpu.make_async_copy(latent, own, load_sem.at[0])
    load.start()

    barrier = pltpu.get_barrier_semaphore()
    near, across = partners_of(tm, row, tm_n, rows_n)
    twin = (tm + 1 - 2 * lax.rem(tm, CORES), row)
    partners = [(tm_at(d), row_at(e)) for e in (-1, 1, 0) for d in (-1, 1)]
    partners = (near + across + partners + [(tm, row_at(e)) for e in (-1, 1)])[::-1]
    for p in partners:
        pl.semaphore_signal(barrier, inc=1, device_id=p, device_id_type=MESH)
    small = [
        pltpu.make_async_copy(src, dst, load_sem.at[1 + n])
        for n, (src, dst) in enumerate(((gain1, g1), (shift1, s1), (gain2, g2), (shift2, s2)))
    ]
    for c in small:
        c.start()
    slot = (0, 4, 2)
    w2_loads, w1_loads = [], []
    for i in range(TAPS):
        w2_loads.append(pltpu.make_async_copy(kernel2.at[i, 0], w2.at[0, :, slot[i]], w2_sem.at[3 * i]))
        w2_loads.append(pltpu.make_async_copy(kernel2.at[i, 1], w2m.at[i], w2_sem.at[3 * i + 1]))
        w2_loads.append(pltpu.make_async_copy(kernel2.at[i, 2], w2.at[1, :, slot[i] + 1], w2_sem.at[3 * i + 2]))
    for i in range(TAPS):
        for k in range(TAPS):
            w1_loads.append(pltpu.make_async_copy(kernel1.at[i, :, k], w1.at[k, i], w1_sem.at[TAPS * i + k]))
    for c in w2_loads + w1_loads:
        c.start()
    load.wait()
    x = lx[2:4, 1:3].astype(jnp.float32).reshape(frames * height * width, cin)
    groups1[...] = member(groups1.shape, cin // GROUPS, 0)
    red_near[0] = pack_stats(x, groups1[...])
    pl.semaphore_wait(barrier, len(partners))

    both = jnp.logical_and
    peers = [
        (next_ok, (tm_at(1), row)),
        (up_ok, (tm, row_at(-1))),
        (down_ok, (tm, row_at(1))),
        (both(next_ok, up_ok), (tm_at(1), row_at(-1))),
        (both(next_ok, down_ok), (tm_at(1), row_at(1))),
    ]
    first_core = lax.rem(tm, CORES) == 0
    arrives = [prev_ok, down_ok, up_ok, both(prev_ok, down_ok), both(prev_ok, up_ok)]

    def exchange(which, sources, targets):
        copies = []
        for n in range(5):
            device = peers[n][1]
            copy = pltpu.make_async_remote_copy(
                src_ref=sources[n], dst_ref=targets[n],
                send_sem=hs_sem.at[which, n], recv_sem=hr_sem.at[which, n],
                device_id=device, device_id_type=MESH,
            )
            copies.append(copy)
        return copies

    def goes(copies, n):
        return both(peers[n][0], jnp.logical_not(first_core)) if copies is halo1 and n >= 3 else peers[n][0]

    def start(copies, which):
        for n in which:
            pl.when(goes(copies, n))(copies[n].start)

    def send(which, ref, n, device):
        pltpu.make_async_remote_copy(
            src_ref=ref.at[0], dst_ref=ref.at[n],
            send_sem=rs_sem.at[which], recv_sem=rr_sem.at[which],
            device_id=device, device_id_type=MESH,
        ).start()

    def arrived(which, ref):
        n = ref.shape[0]
        pltpu.make_async_copy(ref.at[1:n], ref.at[1:n], rr_sem.at[which]).wait()
        parts = ref[...]
        while n > 1:
            n //= 2
            parts = parts[:n] + parts[n:]
        return parts[0]

    def send_all(which, ref, devices):
        for n, device in enumerate(devices):
            send(which, ref, n + 1, device)

    boxes = [(0, 2, 1, 3), (2, 4, 3, 4), (2, 4, 0, 1), (0, 2, 3, 4), (0, 2, 0, 1)]
    halo1 = exchange(
        0,
        [latent, latent.at[:, 0:1], latent.at[:, 1:2], latent.at[:, 0:1], latent.at[:, 1:2]],
        [lx.at[a:b, c:d] for a, b, c, d in boxes],
    )
    send_all(0, red_near, near)
    start(halo1, (1, 2, 3, 4, 0))
    channels1[...] = member(channels1.shape, cin // GROUPS, 1)
    groups2[...] = member(groups2.shape, cout // GROUPS, 0)
    channels2[...] = member(channels2.shape, cout // GROUPS, 1)
    red_across[0] = arrived(0, red_near)
    send_all(1, red_across, across)
    for c in w2_loads:
        c.wait()

    def merge(i):
        for k in range(TAPS):
            mid = w2m[i, k].astype(jnp.float32)
            w2[0, k, slot[i] + 1] = (mid + w2[1, k, slot[i] + 1].astype(jnp.float32)).astype(jnp.bfloat16)
            w2[1, k, slot[i]] = (mid + w2[0, k, slot[i]].astype(jnp.float32)).astype(jnp.bfloat16)

    for i in range(TAPS):
        merge(i)
    forward = []
    for n in (1, 2):
        f0, f1, r0, r1 = boxes[n]
        copy = pltpu.make_async_remote_copy(
            src_ref=lx.at[f0:f1, r0:r1], dst_ref=lx.at[0:2, r0:r1],
            send_sem=hs_sem.at[0, n + 2], recv_sem=hr_sem.at[0, n + 2],
            device_id=twin, device_id_type=MESH,
        )
        pl.when(arrives[n])(halo1[n].wait_recv)
        pl.when(both(arrives[n], first_core))(copy.start)
        forward.append(copy)
    for c in small:
        c.wait()
    count = tm_n * rows_n * frames * height * width * (cin // GROUPS)
    a, b = affine(arrived(1, red_across), count, g1[...], s1[...], channels1[...])

    def normalize(source, target, box, a, b):
        f0, f1, r0, r1 = box
        for f in range(f0, f1):
            for r in range(r0, r1):
                target[f, r] = activate(source[f, r], a, b)

    def normalize_halo(n, copy, source, target, box, a, b):
        f0, f1, r0, r1 = box

        @pl.when(arrives[n])
        def _():
            if copy is not halo1[1] and copy is not halo1[2]:
                copy.wait_recv()
            normalize(source, target, box, a, b)

        @pl.when(jnp.logical_not(arrives[n]))
        def _():
            target[f0:f1, r0:r1] = jnp.zeros((f1 - f0, r1 - r0) + target.shape[2:], target.dtype)

    normalize(lx, xn, (2, 4, 1, 3), a, b)
    for n in range(5):
        normalize_halo(n, halo1[n], lx, xn, boxes[n], a, b)
    for c in w1_loads:
        c.wait()

    size = frames * height * width
    column = lax.rem(lax.broadcasted_iota(jnp.int32, (size, cout), 0), width)
    after = lambda y: jnp.where(column == 0, 0.0, pltpu.roll(y, 1, 0))
    before = lambda y: jnp.where(column == width - 1, 0.0, pltpu.roll(y, size - 1, 0))

    lhs = jnp.concatenate(
        [xn[i : i + frames, j : j + height].reshape(size, cin) for i in range(TAPS) for j in range(TAPS)], axis=1
    )
    y = {
        k: jnp.dot(lhs, w1[k].reshape(TAPS * TAPS * cin, cout), preferred_element_type=jnp.float32)
        for k in (0, 2, 1)
    }
    middle = (after(y[0]) + before(y[2]) + y[1]).astype(jnp.bfloat16)
    mx[1:3, 1:3] = middle.reshape(frames, height, width, cout)

    boxes = [(0, 1, 1, 3), (1, 3, 3, 4), (1, 3, 0, 1), (0, 1, 3, 4), (0, 1, 0, 1)]
    halo2 = exchange(
        1,
        [mx.at[2:3, 1:3], mx.at[1:3, 1:2], mx.at[1:3, 2:3], mx.at[2:3, 1:2], mx.at[2:3, 2:3]],
        [mx.at[a:b, c:d] for a, b, c, d in boxes],
    )
    x = middle.astype(jnp.float32)
    red_all[place] = pack_stats(x, groups2[...])
    @pl.loop(0, tm_n * rows_n - 1)
    def _(n):
        to = n + (place <= n).astype(jnp.int32)
        pltpu.make_async_remote_copy(
            src_ref=red_all.at[place], dst_ref=red_all.at[place],
            send_sem=rs_sem.at[2], recv_sem=rr_sem.at[2],
            device_id=(lax.rem(to, tm_n), lax.div(to, tm_n)), device_id_type=MESH,
        ).start()

    start(halo2, range(5))
    count = tm_n * rows_n * frames * height * width * (cout // GROUPS)
    a, b = affine(arrived(2, red_all), count, g2[...], s2[...], channels2[...])
    normalize(mx, sn, (1, 3, 1, 3), a, b)
    for n in range(5):
        normalize_halo(n, halo2[n], mx, sn, boxes[n], a, b)

    for copies in (halo1, halo2):
        for n in range(5):
            pl.when(goes(copies, n))(copies[n].wait_send)
    for n in (1, 2):
        pl.when(both(arrives[n], first_core))(forward[n - 1].wait_send)
    for which, ref in enumerate((red_near, red_across, red_all)):
        rest = ref.at[1 : ref.shape[0]]
        pltpu.make_async_copy(rest, rest, rs_sem.at[which]).wait()


def second_conv(sn, w2, out, stage, ob, out_sem):
    frames, height, width, cout = sn.shape[0] - 1, sn.shape[1] - 2, sn.shape[2], sn.shape[3]
    size = frames * height * width
    column = lax.rem(lax.broadcasted_iota(jnp.int32, (size, cout), 0), width)
    after = lambda y: jnp.where(column == 0, 0.0, pltpu.roll(y, 1, 0))
    before = lambda y: jnp.where(column == width - 1, 0.0, pltpu.roll(y, size - 1, 0))
    writes = []
    for rb in range(2):
        near = [sn[f : f + 2, r : r + height].reshape(size, cout) for f in (0, 1) for r in (rb, rb + 1)]
        lhs_s = jnp.concatenate(near, axis=1)
        far = [sn[0:3, r : r + height].reshape(3 * height * width, cout) for r in (rb, rb + 1)]
        lhs_r = jnp.concatenate(far, axis=1)
        s, q = {}, {}
        for k in (0, 2, 1):
            s[k] = jnp.dot(lhs_s, w2[rb, k, 0:4].reshape(4 * cout, cout), preferred_element_type=jnp.float32)
            q[k] = jnp.dot(lhs_r, w2[rb, k, 4:6].reshape(2 * cout, cout), preferred_element_type=jnp.float32)
        for ta in range(2):
            skip = ta * height * width
            z = [s[k] + q[k][skip : skip + size] for k in range(TAPS)]
            pair = (after(z[0]) + z[2] + z[1], z[0] + before(z[2]) + z[1])
            for t in range(frames):
                for h in range(height):
                    place = (t * height + h) * width
                    for n in range(cout // LANES):
                        part = slice(n * LANES, (n + 1) * LANES)
                        for tc in range(2):
                            rows = pl.ds(2 * place + tc, width, stride=2)
                            stage[rb, ta, n, rows, :] = pair[tc][place : place + width, part]
                        full = stage[rb, ta, n, 2 * place : 2 * (place + width)]
                        ob[rb, ta, t, h, :, part] = full.astype(jnp.bfloat16)
                    write = pltpu.make_async_copy(
                        ob.at[rb, ta, t, h], out.at[2 * t + ta, 2 * h + rb], out_sem.at[rb, ta, t, h]
                    )
                    write.start()
                    writes.append(write)
    for write in writes:
        write.wait()


def solution(mesh):
    tm_n, rows_n = mesh.shape["tm"], mesh.shape["rows"]

    def per_device(latent, gain1, shift1, kernel1, gain2, shift2, kernel2):
        frames, height, width, cin = latent.shape
        cout = kernel1.shape[-1]
        bf16, f32 = jnp.bfloat16, jnp.float32
        dma = pltpu.SemaphoreType.DMA
        padded, merged = pl.pallas_call(
            functools.partial(kernel, tm_n, rows_n),
            out_shape=(
                pltpu.VMEM((frames + 1, height + 2, width, cout), bf16),
                pltpu.VMEM((2, TAPS, 6, cout, cout), bf16),
            ),
            in_specs=[pl.BlockSpec(memory_space=pltpu.HBM)] * 7,
            out_specs=(pl.BlockSpec(memory_space=pltpu.VMEM),) * 2,
            scratch_shapes=[
                pltpu.VMEM((frames + 2, height + 2, width, cin), bf16),
                pltpu.VMEM((frames + 2, height + 2, width, cin), bf16),
                pltpu.VMEM((TAPS, TAPS, TAPS, cin, cout), bf16),
                pltpu.VMEM((TAPS, TAPS, cout, cout), bf16),
                pltpu.VMEM((frames + 1, height + 2, width, cout), bf16),
                pltpu.VMEM((1, cin), f32),
                pltpu.VMEM((1, cin), f32),
                pltpu.VMEM((1, cout), f32),
                pltpu.VMEM((1, cout), f32),
                pltpu.VMEM((2 * cin, LANES), bf16),
                pltpu.VMEM((LANES, 2 * cin), bf16),
                pltpu.VMEM((2 * cout, LANES), bf16),
                pltpu.VMEM((LANES, 2 * cout), bf16),
                pltpu.VMEM((2 * SIDE * CORES, 1, LANES), f32),
                pltpu.VMEM((2 * tm_n // CORES, 1, LANES), f32),
                pltpu.VMEM((tm_n * rows_n, 1, LANES), f32),
                dma((5,)),
                dma((TAPS * TAPS,)),
                dma((TAPS * TAPS,)),
                dma((2, 5)),
                dma((2, 5)),
                dma((3,)),
                dma((3,)),
            ],
            compiler_params=pltpu.CompilerParams(
                collective_id=0, has_side_effects=True, vmem_limit_bytes=48 * 1024 * 1024
            ),
        )(*(
            pltpu.with_memory_space_constraint(x, pltpu.HBM)
            for x in (
                latent, gain1.reshape(1, -1), shift1.reshape(1, -1), kernel1,
                gain2.reshape(1, -1), shift2.reshape(1, -1), kernel2,
            )
        ))
        return pl.pallas_call(
            second_conv,
            out_shape=pltpu.HBM((2 * frames, 2 * height, 2 * width, cout), bf16),
            in_specs=[pl.BlockSpec(memory_space=pltpu.VMEM)] * 2,
            out_specs=pl.BlockSpec(memory_space=pltpu.HBM),
            scratch_shapes=[
                pltpu.VMEM((2, 2, cout // LANES, 2 * frames * height * width, LANES), f32),
                pltpu.VMEM((2, 2, frames, height, 2 * width, cout), bf16),
                dma((2, 2, frames, height)),
            ],
            compiler_params=pltpu.CompilerParams(vmem_limit_bytes=32 * 1024 * 1024),
        )(padded, merged)

    placed = (P("tm", "rows", None, None), P(), P(), P(), P(), P(), P())
    return jax.shard_map(
        per_device, mesh=mesh, in_specs=placed, out_specs=P("tm", "rows", None, None), check_vma=False
    )
```
